128 devices in a mesh: ctx: 16 (over z, x_lo, core), head: 8 (over y, x_hi).
Axes of the slice: x: 4 (x_hi: 2, x_lo: 2; x = x_hi * 2 + x_lo), y: 4, z: 4, core: 2. Of those that a mesh axis runs over, the one named last changes fastest.
Arguments:
- queries: bfloat16 [8192, 4096], P('ctx', 'head'), may hold values from -5 to 5
- key_rows: bfloat16 [8192, 4096], P('ctx', 'head'), may hold values from -5 to 5
- value_rows: bfloat16 [8192, 4096], P('ctx', 'head'), may hold values from -6 to 6
- out_weight: bfloat16 [4096, 4096], P('head'), may hold values from -0.125 to 0.125
- output_grad: bfloat16 [8192, 4096], P('ctx'), may hold values from -6 to 6
Outputs:
- layer_output: bfloat16 [8192, 4096], P('ctx', 'head')
- query_grad: bfloat16 [8192, 4096], P('ctx', 'head')
- key_grad: bfloat16 [8192, 4096], P('ctx', 'head')
- value_grad: bfloat16 [8192, 4096], P('ctx', 'head')
- weight_grad: bfloat16 [4096, 4096], P('head', 'ctx')
The draws below stay inside these ranges and needn't reach their ends.
All inputs are finite; a program needn't handle non-finite values.
Results may differ from the reference program's by a relative error of at most 0.023.
Values may be sent and summed in bfloat16 or wider, within the bound.
No kernel may reach another device: no remote copies, remote signals or barrier semaphores. Data moves between devices by JAX's collectives and lax.ppermute only.
A program may use at most 192 MiB of HBM per device.

```python
import math
import jax
import jax.numpy as jnp
from jax import lax

D = 4096
HEADS = 32
HD = 128
TOK_DEV = 512
CHANNELS = 4096
TOKENS = 8192
LEVELS = 4
N_CTX = 16
N_HEAD = 8


def draw_queries(key, part):
    key = jax.random.fold_in(key, 11)
    return jax.random.truncated_normal(key, -5.0, 5.0, (TOKENS, CHANNELS), jnp.float32).astype(jnp.bfloat16)


def draw_key_rows(key, part):
    key = jax.random.fold_in(key, 23)
    return jax.random.truncated_normal(key, -5.0, 5.0, (TOKENS, CHANNELS), jnp.float32).astype(jnp.bfloat16)


def with_spikes(drawn, own_key, source, target, parts, factor):
    owner, partner = [(jnp.arange(drawn.shape[position]) // (drawn.shape[position] // parts)).reshape([-1 if axis == position else 1 for axis in range(drawn.ndim)]) for position in (source, target)]
    chosen = jax.random.permutation(own_key, parts)[partner]
    strong = (owner == chosen) | (owner == (partner + parts // 2) % parts)
    return jnp.where(strong, factor * drawn, drawn)


def block_levels(stream_key, dims, cuts, smallest, top_value):
    gain, own = 1.0, jax.random.fold_in(stream_key, 6)
    for axis_at, blocks in cuts:
        heights = jnp.exp(jax.random.uniform(jax.random.fold_in(own, axis_at), (blocks,), jnp.float32, smallest / len(cuts), top_value / len(cuts)))
        gain = gain * jnp.repeat(heights, dims[axis_at] // blocks).reshape([-1 if axis == axis_at else 1 for axis in range(len(dims))])
    return gain


def gaussian(stream_key, dims, spread, bound, cuts=(), dtype=jnp.bfloat16):
    entries = spread * jax.random.normal(stream_key, dims, jnp.float32)
    if cuts:
        entries = entries * block_levels(stream_key, dims, cuts, -0.22, 0.18)
    return jnp.clip(entries, -bound, bound).astype(dtype)


def bell_draw_with(rng, shape, width, bound, cuts, heavy, dtype=jnp.bfloat16):
    drawn = width * jax.random.normal(rng, shape, jnp.float32)
    if cuts:
        drawn = drawn * block_levels(rng, shape, cuts, -0.22, 0.18)
    return jnp.clip(with_spikes(drawn, jax.random.fold_in(rng, 3), *heavy), -bound, bound).astype(dtype)


def setup_inputs(seed: int = 0) -> dict:
    arg_keys = jax.random.split(jax.random.key(seed), 6)
    return {
        "queries": draw_queries(jax.random.fold_in(arg_keys[5], 71), 0),
        "key_rows": draw_key_rows(jax.random.fold_in(arg_keys[5], 71), 0),
        "value_rows": gaussian(arg_keys[2], (TOKENS, CHANNELS), 1.0, 6.0, ((0, 16), (1, 8))),
        "out_weight": bell_draw_with(arg_keys[3], (CHANNELS, D), CHANNELS ** -0.5, 0.125, ((0, 8),), (0, 1, 8, 2.0)),
        "output_grad": bell_draw_with(arg_keys[4], (TOKENS, D), 1.0, 6.0, ((0, 16),), (0, 1, 16, 2.0)),
    }


def pool_pair(row_block):
    row_total, col_total = row_block.shape
    folded = row_block.astype(jnp.float32).reshape(row_total // 2, 2, col_total)
    return ((folded[:, 0] + folded[:, 1]) * 0.5).astype(jnp.bfloat16)

def reference(queries, key_rows, value_rows, out_weight, output_grad):
    score_scale = 1.0 / math.sqrt(HD)
    group_cols = CHANNELS // N_HEAD
    key_levels = [key_rows]
    value_levels = [value_rows]
    for level_idx in range(1, LEVELS):
        key_levels.append(pool_pair(key_levels[-1]))
        value_levels.append(pool_pair(value_levels[-1]))
    key_level_grads = [jnp.zeros(item.shape, jnp.float32) for item in key_levels]
    value_level_grads = [jnp.zeros(item.shape, jnp.float32) for item in value_levels]
    output_blocks = []
    query_blocks = []
    weight_total = jnp.zeros((CHANNELS, D), jnp.float32)
    for block_idx in range(N_CTX):
        row_start = block_idx * TOK_DEV
        places = [(block_idx >> level_idx ^ 1) * TOK_DEV for level_idx in range(LEVELS)]
        key_parts = [key_rows[row_start:row_start + TOK_DEV]]
        value_parts = [value_rows[row_start:row_start + TOK_DEV]]
        for level_idx in range(LEVELS):
            key_parts.append(key_levels[level_idx][places[level_idx]:places[level_idx] + TOK_DEV])
            value_parts.append(value_levels[level_idx][places[level_idx]:places[level_idx] + TOK_DEV])
        query_heads = queries[row_start:row_start + TOK_DEV].astype(jnp.float32).reshape(TOK_DEV, HEADS, HD)
        key_heads = jnp.concatenate(key_parts, axis=0).astype(jnp.float32).reshape(-1, HEADS, HD)
        value_heads = jnp.concatenate(value_parts, axis=0).astype(jnp.float32).reshape(-1, HEADS, HD)
        scores = jnp.einsum('qhd,khd->hqk', query_heads, key_heads) * score_scale
        row_max = lax.optimization_barrier(jnp.max(scores, axis=-1, keepdims=True))
        exp_scores = jnp.exp(scores - row_max)
        attn_probs = exp_scores / lax.optimization_barrier(jnp.sum(exp_scores, axis=-1, keepdims=True))
        probs_low = lax.optimization_barrier(attn_probs.astype(jnp.bfloat16)).astype(jnp.float32)
        attention = jnp.einsum('hqk,khd->qhd', probs_low, value_heads).astype(jnp.bfloat16).reshape(TOK_DEV, CHANNELS)
        partial_value = jnp.zeros((TOK_DEV, D), jnp.float32)
        for group_idx in range(N_HEAD):
            col_lo = group_idx * group_cols
            group_term = jnp.dot(attention[:, col_lo:col_lo + group_cols], out_weight[col_lo:col_lo + group_cols], preferred_element_type=jnp.float32)
            partial_value = partial_value + lax.optimization_barrier(group_term.astype(jnp.bfloat16)).astype(jnp.float32)
        output_blocks.append(partial_value.astype(jnp.bfloat16))
        grad_rows = output_grad[row_start:row_start + TOK_DEV]
        grad_attention = lax.dot_general(grad_rows, out_weight, (((1,), (1,)), ((), ())), preferred_element_type=jnp.float32).astype(jnp.bfloat16)
        block_term = lax.dot_general(attention, grad_rows, (((0,), (0,)), ((), ())), preferred_element_type=jnp.float32)
        weight_total = weight_total + lax.optimization_barrier(block_term.astype(jnp.bfloat16)).astype(jnp.float32)
        grad_heads = grad_attention.astype(jnp.float32).reshape(TOK_DEV, HEADS, HD)
        grad_probs = jnp.einsum('qhd,khd->hqk', grad_heads, value_heads)
        row_dot = lax.optimization_barrier(jnp.sum(attn_probs * grad_probs, axis=-1, keepdims=True))
        grad_scores = lax.optimization_barrier((attn_probs * (grad_probs - row_dot)).astype(jnp.bfloat16)).astype(jnp.float32)
        query_blocks.append((jnp.einsum('hqk,khd->qhd', grad_scores, key_heads) * score_scale).astype(jnp.bfloat16).reshape(TOK_DEV, CHANNELS))
        context_keys = (jnp.einsum('hqk,qhd->khd', grad_scores, query_heads) * score_scale).reshape(-1, CHANNELS)
        context_values = jnp.einsum('hqk,qhd->khd', probs_low, grad_heads).reshape(-1, CHANNELS)
        key_level_grads[0] = key_level_grads[0].at[row_start:row_start + TOK_DEV].add(context_keys[:TOK_DEV])
        value_level_grads[0] = value_level_grads[0].at[row_start:row_start + TOK_DEV].add(context_values[:TOK_DEV])
        for level_idx in range(LEVELS):
            seg_lo = (level_idx + 1) * TOK_DEV
            key_level_grads[level_idx] = key_level_grads[level_idx].at[places[level_idx]:places[level_idx] + TOK_DEV].add(context_keys[seg_lo:seg_lo + TOK_DEV])
            value_level_grads[level_idx] = value_level_grads[level_idx].at[places[level_idx]:places[level_idx] + TOK_DEV].add(context_values[seg_lo:seg_lo + TOK_DEV])
    for level_idx in range(LEVELS - 1, 0, -1):
        key_level_grads[level_idx - 1] = key_level_grads[level_idx - 1] + jnp.repeat(key_level_grads[level_idx], 2, axis=0) * 0.5
        value_level_grads[level_idx - 1] = value_level_grads[level_idx - 1] + jnp.repeat(value_level_grads[level_idx], 2, axis=0) * 0.5
    return (jnp.concatenate(output_blocks, axis=0), jnp.concatenate(query_blocks, axis=0), key_level_grads[0].astype(jnp.bfloat16), value_level_grads[0].astype(jnp.bfloat16), weight_total.astype(jnp.bfloat16))
```

```python
import functools
import math

import jax
import jax.numpy as jnp
from jax import lax
from jax.experimental import pallas as pl
from jax.experimental.pallas import tpu as pltpu
from jax.sharding import PartitionSpec as P

HD = 128
BF = jnp.bfloat16
F32 = jnp.float32
SCALE = 1.0 / math.sqrt(HD)
LOG2E = math.log2(math.e)
VMEM_LIMIT = 56 * 1024 * 1024


def params(**kw):
    return pltpu.CompilerParams(vmem_limit_bytes=VMEM_LIMIT, **kw)


def mm(a, b, dims):
    return lax.dot_general(a, b, (dims, ((), ())), preferred_element_type=F32)


NN = ((1,), (0,))
NT = ((1,), (1,))
TN = ((0,), (0,))


def swap(value, axis, mask):
    size = lax.axis_size(axis)
    return lax.ppermute(value, axis, [(i, i ^ mask) for i in range(size)])


def shape(dims, dtype=BF):
    return jax.ShapeDtypeStruct(dims, dtype)


def grad_attention_kernel(pos, w_ref, g_ref, keep_ref, send_ref, other_ref, acc):
    step = pl.program_id(0)
    core = pos[0]

    @pl.when(step == 0)
    def _():
        acc[...] = jnp.zeros_like(acc)

    acc[...] += mm(w_ref[...], g_ref[...], NT)
    half = g_ref.shape[1] // 2
    for part in range(2):
        away = pl.multiple_of((1 - core) * 256 + part * 512, 256)
        other_ref[:, part * 256 : (part + 1) * 256] = g_ref[:, pl.ds(away, 256)]
    del half

    @pl.when(step == pl.num_programs(0) - 1)
    def _():
        keep_ref[...] = acc[pl.ds(pl.multiple_of(core * 256, 256), 256), :].astype(BF)
        send_ref[...] = acc[pl.ds(pl.multiple_of((1 - core) * 256, 256), 256), :].astype(BF)


def grad_attention_call(pos, out_weight, output_grad):
    width = output_grad.shape[1]
    step = 1024
    return pl.pallas_call(
        grad_attention_kernel,
        grid_spec=pltpu.PrefetchScalarGridSpec(
            num_scalar_prefetch=1,
            grid=(width // step,),
            in_specs=[
                pl.BlockSpec((512, step), lambda i, pos: (0, i)),
                pl.BlockSpec((512, step), lambda i, pos: (0, i)),
            ],
            out_specs=[
                pl.BlockSpec((256, 512), lambda i, pos: (0, 0)),
                pl.BlockSpec((256, 512), lambda i, pos: (0, 0)),
                pl.BlockSpec((512, step // 2), lambda i, pos: (0, i)),
            ],
            scratch_shapes=[pltpu.VMEM((512, 512), F32)],
        ),
        out_shape=[shape((256, 512)), shape((256, 512)), shape((512, width // 2))],
        compiler_params=params(),
        name="grad_attention",
    )(pos, out_weight, output_grad)


def band(rows, cols, ratio, weight, row_major):
    r = lax.broadcasted_iota(jnp.int32, (rows, cols), 0)
    c = lax.broadcasted_iota(jnp.int32, (rows, cols), 1)
    hit = (c // ratio == r) if row_major else (r // ratio == c)
    return jnp.where(hit, weight, 0.0).astype(BF)


def pool_kernel(pos, q_ref, k_ref, v_ref, recv_ref, qt_ref, kv_ref, l1_ref, l2_ref, l3_ref):
    kv_ref[:512, :256] = k_ref[...]
    kv_ref[:512, 256:] = v_ref[...]
    kv_ref[512:, :256] = recv_ref[1]
    kv_ref[512:, 256:] = recv_ref[2]
    fold = band(256, 512, 2, 0.5, True)
    l1_ref[:256, :] = mm(fold, kv_ref[:512, :], NN).astype(BF)
    l1_ref[256:, :] = mm(fold, kv_ref[512:, :], NN).astype(BF)
    l2_ref[...] = mm(fold, l1_ref[...], NN).astype(BF)
    l3_ref[...] = mm(fold[:128, :256], l2_ref[...], NN).astype(BF)
    qt_ref[:, :512] = q_ref[...].T
    qt_ref[:, 512:] = recv_ref[0].T


def pool_call(pos, queries, keys, values, recv):
    own = pl.BlockSpec((512, 256), lambda i, pos: (0, pos[0]))

    def whole(*dims):
        return pl.BlockSpec(dims, lambda i, pos: (0,) * len(dims))

    return pl.pallas_call(
        pool_kernel,
        grid_spec=pltpu.PrefetchScalarGridSpec(
            num_scalar_prefetch=1,
            grid=(1,),
            in_specs=[own, own, own, whole(3, 512, 256)],
            out_specs=[
                whole(256, 1024),
                whole(1024, 512),
                whole(512, 512),
                whole(256, 512),
                whole(128, 512),
            ],
        ),
        out_shape=[
            shape((256, 1024)),
            shape((1024, 512)),
            shape((512, 512)),
            shape((256, 512)),
            shape((128, 512)),
        ],
        compiler_params=params(),
        name="pool",
    )(pos, queries, keys, values, recv)


def score_block(key, value, qt_ref, e_ref, slot, carry):
    new = []
    for c, (m_run, l_run, acc) in enumerate(carry):
        cols = slice(c * QC, (c + 1) * QC)
        s = mm(key, qt_ref[:, cols], NN)
        m = jnp.max(s, axis=0, keepdims=True) * (SCALE * LOG2E)
        e = jnp.exp2(s * (SCALE * LOG2E) - m)
        l = jnp.sum(e, axis=0, keepdims=True)
        e_low = e.astype(BF)
        e_ref[0, slot, :, cols] = e_low
        u = mm(value, e_low, TN)
        if m_run is None:
            new.append((m, l, u, m))
        else:
            top = jnp.maximum(m_run, m)
            f_run, f_new = jnp.exp2(m_run - top), jnp.exp2(m - top)
            new.append((top, l_run * f_run + l * f_new, acc * f_run + u * f_new, m))
    return new


QC = 512
NQ = 2


def near_kernel(qt_ref, kv_k, kv_v, e_ref, acc_ref, st_ref):
    carry = [(None, None, None)] * NQ
    tops = []
    for j in range(2):
        rows = slice(j * 512, (j + 1) * 512)
        got = score_block(kv_k[rows, :], kv_v[rows, :], qt_ref, e_ref, j, carry)
        carry = [g[:3] for g in got]
        tops.append([g[3] for g in got])
    for c in range(NQ):
        cols = slice(c * QC, (c + 1) * QC)
        m, l, acc = carry[c]
        acc_ref[:, cols] = acc
        st_ref[0, 0:1, cols] = m
        st_ref[0, 1:2, cols] = l
        st_ref[0, 2:3, cols] = tops[0][c]
        st_ref[0, 3:4, cols] = tops[1][c]


def near_call(qt, kv):
    return pl.pallas_call(
        near_kernel,
        grid=(2,),
        in_specs=[
            pl.BlockSpec((128, 1024), lambda h: (h, 0)),
            pl.BlockSpec((1024, 128), lambda h: (0, h)),
            pl.BlockSpec((1024, 128), lambda h: (0, h + 2)),
        ],
        out_specs=[
            pl.BlockSpec((1, 2, 512, 1024), lambda h: (h, 0, 0, 0)),
            pl.BlockSpec((128, 1024), lambda h: (h, 0)),
            pl.BlockSpec((1, 8, 1024), lambda h: (h, 0, 0)),
        ],
        out_shape=[
            shape((2, 2, 512, 1024)),
            shape((256, 1024), F32),
            shape((2, 8, 1024), F32),
        ],
        compiler_params=params(),
        name="near_scores",
    )(qt, kv, kv)


FAR_ROWS = (512, 256, 256, 128, 128, 128, 128)


def gather_far(refs, dst):
    at = 0
    for ref, rows in zip(refs, FAR_ROWS):
        dst[at : at + rows, :] = ref[...]
        at += rows


def far_kernel(qt_ref, *refs):
    keys, values = refs[:7], refs[7:14]
    acc_ref, st_ref, e_ref, o_ref, s_ref, k_all, v_all = refs[14:]
    gather_far(keys, k_all)
    gather_far(values, v_all)
    carry = []
    for c in range(NQ):
        cols = slice(c * QC, (c + 1) * QC)
        carry.append((st_ref[0, 0:1, cols], st_ref[0, 1:2, cols], acc_ref[:, cols]))
    tops = [[st_ref[0, 2 + j : 3 + j, c * QC : (c + 1) * QC] for c in range(NQ)] for j in range(2)]
    for j in range(3):
        rows = slice(j * 512, (j + 1) * 512)
        got = score_block(k_all[rows, :], v_all[rows, :], qt_ref, e_ref, j, carry)
        carry = [g[:3] for g in got]
        tops.append([g[3] for g in got])
    for c in range(NQ):
        cols = slice(c * QC, (c + 1) * QC)
        m, l, acc = carry[c]
        inv = 1.0 / l
        o_ref[:, cols] = (acc * inv).astype(BF)
        for j in range(5):
            s_ref[0, j : j + 1, cols] = jnp.exp2(tops[j][c] - m) * inv


def far_specs(offset):
    return [pl.BlockSpec((rows, 128), functools.partial(lambda o, h: (0, h + o), offset)) for rows in FAR_ROWS]


def far_call(qt, far, acc, stats):
    return pl.pallas_call(
        far_kernel,
        grid=(2,),
        in_specs=[
            pl.BlockSpec((128, 1024), lambda h: (h, 0)),
            *far_specs(0),
            *far_specs(2),
            pl.BlockSpec((128, 1024), lambda h: (h, 0)),
            pl.BlockSpec((1, 8, 1024), lambda h: (h, 0, 0)),
        ],
        out_specs=[
            pl.BlockSpec((1, 3, 512, 1024), lambda h: (h, 0, 0, 0)),
            pl.BlockSpec((128, 1024), lambda h: (h, 0)),
            pl.BlockSpec((1, 8, 1024), lambda h: (h, 0, 0)),
        ],
        out_shape=[
            shape((2, 3, 512, 1024)),
            shape((256, 1024)),
            shape((2, 8, 1024), F32),
        ],
        scratch_shapes=[pltpu.VMEM((1536, 128), BF), pltpu.VMEM((1536, 128), BF)],
        compiler_params=params(),
        name="far_scores",
    )(qt, *far, *far, acc, stats)


def project_kernel(pos, o_ref, r_ref, w_mine, w_other, a0, a1, a2, a3, b0, b1, mine, other):
    step = pl.program_id(0)

    @pl.when(step == 0)
    def _():
        mine[...] = o_ref[:, :512].T
        other[...] = r_ref[:, 512:].T

    out = (mm(mine[...], w_mine[...], NN) + mm(other[...], w_other[...], NN)).astype(BF)
    for dy, a in enumerate((a0, a1, a2, a3)):
        for dx, b in enumerate((b0, b1)):

            @pl.when(step == ORDER.index((dy, dx)))
            def _():
                a[:, dx * 512 : (dx + 1) * 512] = out[:256]
                b[dy] = out[256:]


ORDER = [(2, 1), (1, 1), (3, 1), (0, 1), (2, 0), (1, 0), (3, 0), (0, 0)]


def project_target(i):
    dy = jnp.where(i % 4 == 0, 2, jnp.where(i % 4 == 1, 1, jnp.where(i % 4 == 2, 3, 0)))
    dx = 1 - i // 4
    return dy * 2 + dx


def project_call(pos, attn, attn_other, out_weight):
    def whole(*dims):
        return pl.BlockSpec(dims, lambda i, pos: (0,) * len(dims))

    def weight(flip):
        return pl.BlockSpec(
            (256, 512), lambda i, pos: (pos[0] ^ flip, pos[1] ^ project_target(i))
        )

    return pl.pallas_call(
        project_kernel,
        grid_spec=pltpu.PrefetchScalarGridSpec(
            num_scalar_prefetch=1,
            grid=(8,),
            in_specs=[whole(256, 1024), whole(256, 1024), weight(0), weight(1)],
            out_specs=[whole(256, 1024)] * 4 + [whole(4, 256, 512)] * 2,
            scratch_shapes=[pltpu.VMEM((512, 256), BF), pltpu.VMEM((512, 256), BF)],
        ),
        out_shape=[shape((256, 1024))] * 4 + [shape((4, 256, 512))] * 2,
        compiler_params=params(),
        name="project",
    )(pos, attn, attn_other, out_weight, out_weight)


def weight_kernel(pos, o_ref, r_ref, g_own, g_recv, w0, w1, w2, w3):
    step = pl.program_id(0)
    core = pos[0]
    own, far = g_own[...], g_recv[...]
    up = (mm(o_ref[:, :512], own, NN) + mm(o_ref[:, 512:], far, NN)).astype(BF)
    down = (mm(r_ref[:, 512:], own, NN) + mm(r_ref[:, :512], far, NN)).astype(BF)
    first = pl.ds(pl.multiple_of(core * 256, 256), 256)
    second = pl.ds(pl.multiple_of((1 - core) * 256, 256), 256)
    for dz, w in enumerate((w0, w1, w2, w3)):

        @pl.when(step // 2 == dz)
        def _():
            w[step % 2, first, :] = up
            w[step % 2, second, :] = down


def weight_call(pos, attn, attn_other, output_grad, grad_recv):
    def whole(*dims):
        return pl.BlockSpec(dims, lambda i, pos: (0,) * len(dims))

    return pl.pallas_call(
        weight_kernel,
        grid_spec=pltpu.PrefetchScalarGridSpec(
            num_scalar_prefetch=1,
            grid=(8,),
            in_specs=[
                whole(256, 1024),
                whole(256, 1024),
                pl.BlockSpec((512, 256), lambda i, pos: (0, (pos[2] ^ i) * 2 + pos[0])),
                pl.BlockSpec((512, 256), lambda i, pos: (0, pos[2] ^ i)),
            ],
            out_specs=[whole(2, 512, 256)] * 4,
        ),
        out_shape=[shape((2, 512, 256))] * 4,
        compiler_params=params(),
        name="weight_term",
    )(pos, attn, attn_other, output_grad, grad_recv)


def grad_block(key, value, qt, da, row_dot, s, e_ref, slot, ds_ref, dq_ref, first):
    da_low = (da * s).astype(BF)
    dot_scaled = row_dot * s
    for c in range(NQ):
        cols = slice(c * QC, (c + 1) * QC)
        dp = mm(value, da_low[:, cols], NN)
        ds = (e_ref[0, slot, :, cols].astype(F32) * (dp - dot_scaled[:, cols])).astype(BF)
        ds_ref[:, cols] = ds
        part = mm(key, ds, TN)
        if first:
            dq_ref[:, cols] = part
        else:
            dq_ref[:, cols] += part
    dk = mm(ds_ref[...], qt, NT) * SCALE
    dv = mm(e_ref[0, slot], da_low, NT)
    return dk, dv


def grad_rows(da_own, da_recv, o_ref):
    da = jnp.concatenate([da_own[...], da_recv[...]], axis=1).astype(F32)
    return da, jnp.sum(da * o_ref[...].astype(F32), axis=0, keepdims=True)


def far_grad_kernel(qt_ref, da_own, da_recv, o_ref, s_ref, e_ref, *refs):
    keys, values = refs[:7], refs[7:14]
    outs = refs[14:21]
    dq_ref, k_all, v_all, ds_ref = refs[21:]
    head = pl.program_id(0)
    gather_far(keys, k_all)
    gather_far(values, v_all)
    da, row_dot = grad_rows(da_own, da_recv, o_ref)
    k_cols = pl.ds(pl.multiple_of(head * 128, 128), 128)
    v_cols = pl.ds(pl.multiple_of(head * 128 + 256, 128), 128)
    qt = qt_ref[...]
    at = 0
    for j in range(3):
        rows = slice(j * 512, (j + 1) * 512)
        s = s_ref[0, 2 + j : 3 + j, :]
        dk, dv = grad_block(
            k_all[rows, :], v_all[rows, :], qt, da, row_dot, s, e_ref, j, ds_ref, dq_ref, j == 0
        )
        lo = 0
        while lo < 512:
            n = FAR_ROWS[at]
            outs[at][:, k_cols] = dk[lo : lo + n].astype(BF)
            outs[at][:, v_cols] = dv[lo : lo + n].astype(BF)
            lo += n
            at += 1


def common_specs():
    return [
        pl.BlockSpec((128, 1024), lambda h: (h, 0)),
        pl.BlockSpec((128, 512), lambda h: (h, 0)),
        pl.BlockSpec((128, 512), lambda h: (h, 0)),
        pl.BlockSpec((128, 1024), lambda h: (h, 0)),
        pl.BlockSpec((1, 8, 1024), lambda h: (h, 0, 0)),
    ]


def far_grad_call(qt, da_own, da_recv, attn, scales, e_far, far):
    return pl.pallas_call(
        far_grad_kernel,
        grid=(2,),
        in_specs=[
            *common_specs(),
            pl.BlockSpec((1, 3, 512, 1024), lambda h: (h, 0, 0, 0)),
            *far_specs(0),
            *far_specs(2),
        ],
        out_specs=[pl.BlockSpec((rows, 512), lambda h: (0, 0)) for rows in FAR_ROWS]
        + [pl.BlockSpec((128, 1024), lambda h: (h, 0))],
        out_shape=[shape((rows, 512)) for rows in FAR_ROWS] + [shape((256, 1024), F32)],
        scratch_shapes=[
            pltpu.VMEM((1536, 128), BF),
            pltpu.VMEM((1536, 128), BF),
            pltpu.VMEM((512, 1024), BF),
        ],
        compiler_params=params(),
        name="far_grads",
    )(qt, da_own, da_recv, attn, scales, e_far, *far, *far)


def near_grad_kernel(
    qt_ref, da_own, da_recv, o_ref, s_ref, e_ref, kv_k, kv_v, dq_in, kv_ref, q_own, q_send, ds_ref, dq_ref
):
    head = pl.program_id(0)
    da, row_dot = grad_rows(da_own, da_recv, o_ref)
    k_cols = pl.ds(pl.multiple_of(head * 128, 128), 128)
    v_cols = pl.ds(pl.multiple_of(head * 128 + 256, 128), 128)
    qt = qt_ref[...]
    dq_ref[...] = dq_in[...]
    for j in range(2):
        rows = slice(j * 512, (j + 1) * 512)
        s = s_ref[0, j : j + 1, :]
        dk, dv = grad_block(
            kv_k[rows, :], kv_v[rows, :], qt, da, row_dot, s, e_ref, j, ds_ref, dq_ref, False
        )
        kv_ref[rows, k_cols] = dk
        kv_ref[rows, v_cols] = dv
    q_own[...] = (dq_ref[:, :512] * SCALE).T.astype(BF)
    q_send[...] = (dq_ref[:, 512:] * SCALE).T.astype(BF)


def near_grad_call(qt, da_own, da_recv, attn, scales, e_near, kv, dq):
    return pl.pallas_call(
        near_grad_kernel,
        grid=(2,),
        in_specs=[
            *common_specs(),
            pl.BlockSpec((1, 2, 512, 1024), lambda h: (h, 0, 0, 0)),
            pl.BlockSpec((1024, 128), lambda h: (0, h)),
            pl.BlockSpec((1024, 128), lambda h: (0, h + 2)),
            pl.BlockSpec((128, 1024), lambda h: (h, 0)),
        ],
        out_specs=[
            pl.BlockSpec((1024, 512), lambda h: (0, 0)),
            pl.BlockSpec((512, 128), lambda h: (0, h)),
            pl.BlockSpec((512, 128), lambda h: (0, h)),
        ],
        out_shape=[shape((1024, 512), F32), shape((512, 256)), shape((512, 256))],
        scratch_shapes=[pltpu.VMEM((512, 1024), BF), pltpu.VMEM((128, 1024), F32)],
        compiler_params=params(),
        name="near_grads",
    )(qt, da_own, da_recv, attn, scales, e_near, kv, kv, dq)


def collect_kernel(kv_ref, *refs):
    back, own_ref, send_ref = refs[:7], refs[7], refs[8]
    for part, out in ((1, send_ref), (0, own_ref)):
        total = kv_ref[part * 512 : (part + 1) * 512, :]
        for level, group in ((1, back[:1]), (2, back[1:3]), (3, back[3:])):
            n = 512 >> level
            rows = slice(part * n, (part + 1) * n)
            spread = band(512, n, 1 << level, 0.5**level, False)
            for ref in group:
                total = total + mm(spread, ref[rows, :], NN)
        out[...] = total.astype(BF)


def collect_call(kv_grad, back):
    def whole(*dims):
        return pl.BlockSpec(dims, lambda i: (0,) * len(dims))

    return pl.pallas_call(
        collect_kernel,
        grid=(1,),
        in_specs=[whole(1024, 512)] + [whole(rows, 512) for rows in FAR_ROWS],
        out_specs=[whole(512, 512)] * 2,
        out_shape=[shape((512, 512))] * 2,
        compiler_params=params(),
        name="collect",
    )(kv_grad, *back)


def place_kernel(pos, q_own, q_recv, kv_own, kv_recv, q_out, k_out, v_out):
    mine = pl.ds(pl.multiple_of(pos[0] * 256, 256), 256)
    other = pl.ds(pl.multiple_of((1 - pos[0]) * 256, 256), 256)
    q_out[:, mine] = q_own[...]
    q_out[:, other] = q_recv[...]
    k_out[:, mine] = kv_own[:, :256]
    k_out[:, other] = kv_recv[:, :256]
    v_out[:, mine] = kv_own[:, 256:]
    v_out[:, other] = kv_recv[:, 256:]


def place_call(pos, q_own, q_recv, kv_own, kv_recv):
    def whole(*dims):
        return pl.BlockSpec(dims, lambda i, pos: (0,) * len(dims))

    return pl.pallas_call(
        place_kernel,
        grid_spec=pltpu.PrefetchScalarGridSpec(
            num_scalar_prefetch=1,
            grid=(1,),
            in_specs=[whole(512, 256)] * 2 + [whole(512, 512)] * 2,
            out_specs=[whole(512, 512)] * 3,
        ),
        out_shape=[shape((512, 512))] * 3,
        compiler_params=params(),
        name="place",
    )(pos, q_own, q_recv, kv_own, kv_recv)


FAR_MASKS = (2, 4, 6, 8, 10, 12, 14)


def add(*terms):
    return functools.reduce(jnp.add, [t.astype(F32) for t in terms])


def shards(queries, key_rows, value_rows, out_weight, output_grad):
    ctx = lax.axis_index("ctx")
    core = ctx % 2
    pos = jnp.stack([core, lax.axis_index("head"), ctx // 2]).astype(jnp.int32)

    away = [
        lax.dynamic_slice_in_dim(a, (1 - core) * 256, 256, axis=1)
        for a in (queries, key_rows, value_rows)
    ]
    recv = swap(jnp.stack(away), "ctx", 1)
    da_own, da_send, grad_send = grad_attention_call(pos, out_weight, output_grad)
    da_recv = swap(da_send, "ctx", 1)
    grad_recv = swap(grad_send, "ctx", 1)

    qt, kv, l1, l2, l3 = pool_call(pos, queries, key_rows, value_rows, recv)
    pooled = (l1, l2, l2, l3, l3, l3, l3)
    far = [swap(a, "ctx", mask) for a, mask in zip(pooled, FAR_MASKS)]
    e_near, acc, stats = near_call(qt, kv)
    e_far, attn, scales = far_call(qt, far, acc, stats)

    attn_other = swap(attn, "ctx", 1)
    a0, a1, a2, a3, b0, b1 = project_call(pos, attn, attn_other, out_weight)
    b_recv = swap(b1, "head", 1)
    a_recv = [swap(a, "head", 2 * dy) for dy, a in ((1, a1), (2, a2), (3, a3))]

    w_parts = weight_call(pos, attn, attn_other, output_grad, grad_recv)
    w_recv = [swap(w_parts[dz], "ctx", 4 * dz) for dz in (1, 2, 3)]

    *level_grads, dq = far_grad_call(qt, da_own, da_recv, attn, scales, e_far, far)
    back = [swap(g, "ctx", mask) for g, mask in zip(level_grads, FAR_MASKS)]
    kv_grad, q_own, q_send = near_grad_call(qt, da_own, da_recv, attn, scales, e_near, kv, dq)
    q_recv = swap(q_send, "ctx", 1)

    b_sum = add(b0, b_recv)
    b_back = [swap(b_sum[dy].astype(BF), "head", 2 * dy) for dy in (1, 2, 3)]
    a_sum = add(a0, *a_recv)
    a_back = swap(a_sum[:, 512:].astype(BF), "head", 1)
    w_sum = add(w_parts[0], *w_recv)
    w_back = swap(w_sum[1].astype(BF), "ctx", 2)

    layer_output = jnp.concatenate(
        [add(a_sum[:, :512], a_back), add(b_sum[0], *b_back)], axis=0
    ).astype(BF)
    weight_grad = add(w_sum[0], w_back).astype(BF)

    kv_own, kv_send = collect_call(kv_grad, back)
    kv_recv = swap(kv_send, "ctx", 1)
    query_grad, key_grad, value_grad = place_call(pos, q_own, q_recv, kv_own, kv_recv)
    return (layer_output, query_grad, key_grad, value_grad, weight_grad)


def solution(mesh):
    placed = (P("ctx", "head"), P("ctx", "head"), P("ctx", "head"), P("head", None), P("ctx", None))
    return jax.shard_map(
        shards,
        mesh=mesh,
        in_specs=placed,
        out_specs=(
            P("ctx", "head"),
            P("ctx", "head"),
            P("ctx", "head"),
            P("ctx", "head"),
            P("head", "ctx"),
        ),
        check_vma=False,
    )
```

```python
import functools
import math

import jax
import jax.numpy as jnp
from jax import lax
from jax.experimental import pallas as pl
from jax.experimental.pallas import tpu as pltpu
from jax.sharding import PartitionSpec as P

HD = 128
BF = jnp.bfloat16
F32 = jnp.float32
SCALE = 1.0 / math.sqrt(HD)
LOG2E = math.log2(math.e)
VMEM_LIMIT = 16 * 1024 * 1024


def cost(us):
    return pl.CostEstimate(flops=0, bytes_accessed=int(us * 1.20e+06), transcendentals=0)


def params(**kw):
    return pltpu.CompilerParams(vmem_limit_bytes=VMEM_LIMIT, **kw)


def mm(a, b, dims):
    return lax.dot_general(a, b, (dims, ((), ())), preferred_element_type=F32)


NN = ((1,), (0,))
NT = ((1,), (1,))
TN = ((0,), (0,))


def swap(value, axis, mask):
    size = lax.axis_size(axis)
    return lax.ppermute(value, axis, [(i, i ^ mask) for i in range(size)])


def shape(dims, dtype=BF):
    return jax.ShapeDtypeStruct(dims, dtype)


def grad_attention_kernel(pos, w_ref, g_ref, keep_ref, send_ref, other_ref, acc):
    step = pl.program_id(0)
    core = pos[0]

    @pl.when(step == 0)
    def _():
        acc[...] = jnp.zeros_like(acc)

    acc[...] += mm(w_ref[...], g_ref[...], NT)
    for part in range(2):
        away = pl.multiple_of((1 - core) * 256 + part * 512, 256)
        other_ref[:, part * 256 : (part + 1) * 256] = g_ref[:, pl.ds(away, 256)]

    @pl.when(step == pl.num_programs(0) - 1)
    def _():
        keep_ref[...] = acc[pl.ds(pl.multiple_of(core * 256, 256), 256), :].astype(BF)
        send_ref[...] = acc[pl.ds(pl.multiple_of((1 - core) * 256, 256), 256), :].astype(BF)


def grad_attention_call(pos, out_weight, output_grad):
    width = output_grad.shape[1]
    step = 1024
    return pl.pallas_call(
        grad_attention_kernel,
        grid_spec=pltpu.PrefetchScalarGridSpec(
            num_scalar_prefetch=1,
            grid=(width // step,),
            in_specs=[
                pl.BlockSpec((512, step), lambda i, pos: (0, i)),
                pl.BlockSpec((512, step), lambda i, pos: (0, i)),
            ],
            out_specs=[
                pl.BlockSpec((256, 512), lambda i, pos: (0, 0)),
                pl.BlockSpec((256, 512), lambda i, pos: (0, 0)),
                pl.BlockSpec((512, step // 2), lambda i, pos: (0, i)),
            ],
            scratch_shapes=[pltpu.VMEM((512, 512), F32)],
        ),
        out_shape=[shape((256, 512)), shape((256, 512)), shape((512, width // 2))],
        compiler_params=params(),
        cost_estimate=cost(4.5),
        name="grad_attention",
    )(pos, out_weight, output_grad)


def band(rows, cols, ratio, weight, row_major):
    r = lax.broadcasted_iota(jnp.int32, (rows, cols), 0)
    c = lax.broadcasted_iota(jnp.int32, (rows, cols), 1)
    hit = (c // ratio == r) if row_major else (r // ratio == c)
    return jnp.where(hit, weight, 0.0).astype(BF)


def prepare_kernel(pos, q_ref, k_ref, v_ref, qt_ref, kv_ref, l1_ref):
    fold = band(256, 512, 2, 0.5, True)
    for at, ref in enumerate((k_ref, v_ref)):
        cols = slice(at * 256, (at + 1) * 256)
        kv_ref[:, cols] = ref[...]
        l1_ref[:, cols] = mm(fold, ref[...], NN).astype(BF)
    qt_ref[...] = q_ref[...].T


def pool_kernel(pos, k_ref, v_ref, own_ref, kv_ref, l1_ref):
    fold = band(256, 512, 2, 0.5, True)
    l1_ref[:256, :] = own_ref[...]
    for at, ref in enumerate((k_ref, v_ref)):
        cols = slice(at * 256, (at + 1) * 256)
        kv_ref[:, cols] = ref[...]
        l1_ref[256:, cols] = mm(fold, ref[...], NN).astype(BF)


def whole(*dims):
    return pl.BlockSpec(dims, lambda i, pos: (0,) * len(dims))


def half_cols():
    return pl.BlockSpec((512, 256), lambda i, pos: (0, pos[0]))


def prepare_call(pos, queries, keys, values):
    return pl.pallas_call(
        prepare_kernel,
        grid_spec=pltpu.PrefetchScalarGridSpec(
            num_scalar_prefetch=1,
            grid=(1,),
            in_specs=[half_cols()] * 3,
            out_specs=[whole(256, 512), whole(512, 512), whole(256, 512)],
        ),
        out_shape=[shape((256, 512)), shape((512, 512)), shape((256, 512))],
        compiler_params=params(),
        cost_estimate=cost(1.0),
        name="prepare",
    )(pos, queries, keys, values)


def pool_call(pos, keys, values, l1_own):
    return pl.pallas_call(
        pool_kernel,
        grid_spec=pltpu.PrefetchScalarGridSpec(
            num_scalar_prefetch=1,
            grid=(1,),
            in_specs=[half_cols(), half_cols(), whole(256, 512)],
            out_specs=[whole(512, 512), whole(512, 512)],
        ),
        out_shape=[shape((512, 512)), shape((512, 512))],
        compiler_params=params(),
        cost_estimate=cost(1.0),
        name="pool",
    )(pos, keys, values, l1_own)


def pool_more_kernel(pos, l1_ref, own_ref, q_ref, l2_ref, l3_ref, qt_ref):
    fold = band(256, 512, 2, 0.5, True)
    l2 = mm(fold, l1_ref[...], NN).astype(BF)
    l2_ref[...] = l2
    l3_ref[...] = mm(fold[:128, :256], l2, NN).astype(BF)
    qt_ref[:, :512] = own_ref[...]
    qt_ref[:, 512:] = q_ref[...].T


def pool_more_call(pos, l1, qt_own, queries):
    return pl.pallas_call(
        pool_more_kernel,
        grid_spec=pltpu.PrefetchScalarGridSpec(
            num_scalar_prefetch=1,
            grid=(1,),
            in_specs=[whole(512, 512), whole(256, 512), half_cols()],
            out_specs=[whole(256, 512), whole(128, 512), whole(256, 1024)],
        ),
        out_shape=[shape((256, 512)), shape((128, 512)), shape((256, 1024))],
        compiler_params=params(),
        cost_estimate=cost(1.0),
        name="pool_more",
    )(pos, l1, qt_own, queries)


def score_block(key, value, qt_ref, e_ref, slot, carry):
    new = []
    for c, (m_run, l_run, acc) in enumerate(carry):
        cols = slice(c * QC, (c + 1) * QC)
        s = mm(key, qt_ref[:, cols], NN)
        m = jnp.max(s, axis=0, keepdims=True) * (SCALE * LOG2E)
        e = jnp.exp2(s * (SCALE * LOG2E) - m)
        l = jnp.sum(e, axis=0, keepdims=True)
        e_low = e.astype(BF)
        e_ref[0, slot, :, cols] = e_low
        u = mm(value, e_low, TN)
        if m_run is None:
            new.append((m, l, u, m))
        else:
            top = jnp.maximum(m_run, m)
            f_run, f_new = jnp.exp2(m_run - top), jnp.exp2(m - top)
            new.append((top, l_run * f_run + l * f_new, acc * f_run + u * f_new, m))
    return new


QC = 1024
NQ = 1


def near_kernel(qt_ref, *refs):
    keys, values = refs[:2], refs[2:4]
    e_ref, acc_ref, st_ref = refs[4:]
    carry = [(None, None, None)] * NQ
    for j in range(2):
        got = score_block(keys[j][...], values[j][...], qt_ref, e_ref, j, carry)
        carry = [g[:3] for g in got]
        for c in range(NQ):
            st_ref[0, 2 + j : 3 + j, c * QC : (c + 1) * QC] = got[c][3]
    put_carry(carry, acc_ref, st_ref)


def put_carry(carry, acc_ref, st_ref):
    for c, (m, l, acc) in enumerate(carry):
        cols = slice(c * QC, (c + 1) * QC)
        acc_ref[:, cols] = acc
        st_ref[0, 0:1, cols] = m
        st_ref[0, 1:2, cols] = l


def get_carry(acc_ref, st_ref):
    parts = [slice(c * QC, (c + 1) * QC) for c in range(NQ)]
    return [(st_ref[0, 0:1, p], st_ref[0, 1:2, p], acc_ref[:, p]) for p in parts]


def middle_kernel(qt_ref, *refs):
    keys, values = refs[:2], refs[2:4]
    acc_in, st_in, e_ref, acc_ref, st_ref = refs[4:]
    carry = get_carry(acc_in, st_in)
    st_ref[0, 2:4, :] = st_in[0, 2:4, :]
    for j in range(2):
        got = score_block(keys[j][...], values[j][...], qt_ref, e_ref, j, carry)
        carry = [g[:3] for g in got]
        for c in range(NQ):
            st_ref[0, 4 + j : 5 + j, c * QC : (c + 1) * QC] = got[c][3]
    put_carry(carry, acc_ref, st_ref)


def last_kernel(qt_ref, key, value, acc_in, st_in, e_ref, o_ref, s_ref):
    got = score_block(key[...], value[...], qt_ref, e_ref, 0, get_carry(acc_in, st_in))
    for c, (m, l, acc, top) in enumerate(got):
        cols = slice(c * QC, (c + 1) * QC)
        inv = 1.0 / l
        o_ref[:, cols] = (acc * inv).astype(BF)
        s_ref[0, :4, cols] = jnp.exp2(st_in[0, 2:6, cols] - m) * inv
        s_ref[0, 4:5, cols] = jnp.exp2(top - m) * inv


def per_head(*dims):
    return pl.BlockSpec(dims, lambda h: (h,) + (0,) * (len(dims) - 1))


def kv_specs(count):
    def spec(offset):
        return pl.BlockSpec((512, 128), lambda h: (0, h + offset))

    return [spec(0)] * count + [spec(2)] * count


CARRY_SPECS = [per_head(128, 1024), per_head(1, 8, 1024)]
CARRY = [shape((256, 1024), F32), shape((2, 8, 1024), F32)]


def score_call(kernel, name, us, qt, blocks, carry, last=False):
    n = len(blocks)
    return pl.pallas_call(
        kernel,
        grid=(2,),
        in_specs=[per_head(128, 1024), *kv_specs(n), *CARRY_SPECS[: len(carry)]],
        out_specs=[per_head(1, n, 512, 1024), *CARRY_SPECS],
        out_shape=[
            shape((2, n, 512, 1024)),
            shape((256, 1024)) if last else CARRY[0],
            CARRY[1],
        ],
        compiler_params=params(),
        cost_estimate=cost(us),
        name=name,
    )(qt, *blocks, *blocks, *carry)


def project_kernel(
    pos, o_ref, r_ref, w_mine, w_other, keep, first_1, first_3, late_1, late_3, mine, other
):
    step = pl.program_id(0)

    @pl.when(step == 0)
    def _():
        mine[...] = o_ref[:, :512].T
        other[...] = r_ref[:, 512:].T

    out = (mm(mine[...], w_mine[...], NN) + mm(other[...], w_other[...], NN)).astype(BF)
    top, low = out[:256], out[256:]

    @pl.when(step == 0)
    def _():
        keep[...] = out

    @pl.when(step == 1)
    def _():
        first_1[256:] = top
        late_1[...] = low

    @pl.when(step == 2)
    def _():
        first_1[:256] = top
        first_3[:256] = low

    @pl.when(step == 3)
    def _():
        first_3[256:] = low
        late_3[...] = top


def project_call(pos, attn, attn_other, out_weight, dx):
    def weight(flip):
        return pl.BlockSpec((256, 512), lambda i, pos: (pos[0] ^ flip, pos[1] ^ (i * 2 + dx)))

    return pl.pallas_call(
        project_kernel,
        grid_spec=pltpu.PrefetchScalarGridSpec(
            num_scalar_prefetch=1,
            grid=(4,),
            in_specs=[whole(256, 1024), whole(256, 1024), weight(0), weight(1)],
            out_specs=[whole(512, 512)] * 3 + [whole(256, 512)] * 2,
            scratch_shapes=[pltpu.VMEM((512, 256), BF), pltpu.VMEM((512, 256), BF)],
        ),
        out_shape=[shape((512, 512))] * 3 + [shape((256, 512))] * 2,
        compiler_params=params(),
        cost_estimate=cost(3.0),
        name="project",
    )(pos, attn, attn_other, out_weight, out_weight)


def weight_kernel(
    pos, o_ref, r_ref, g_own, g_recv, keep, first_1, first_3, late_1, late_3
):
    dz, dx = pl.program_id(0) // 2, pl.program_id(0) % 2
    own, far = g_own[...], g_recv[...]
    up = (mm(o_ref[:, :512], own, NN) + mm(o_ref[:, 512:], far, NN)).astype(BF)
    down = (mm(r_ref[:, 512:], own, NN) + mm(r_ref[:, :512], far, NN)).astype(BF)

    @pl.when(dz == 0)
    def _():
        keep[0, dx] = up
        keep[1, dx] = down

    @pl.when(dz == 1)
    def _():
        first_1[1, dx] = up
        late_1[dx] = down

    @pl.when(dz == 2)
    def _():
        first_1[0, dx] = up
        first_3[0, dx] = down

    @pl.when(dz == 3)
    def _():
        first_3[1, dx] = down
        late_3[dx] = up


def weight_call(pos, attn, attn_other, output_grad, grad_recv):
    return pl.pallas_call(
        weight_kernel,
        grid_spec=pltpu.PrefetchScalarGridSpec(
            num_scalar_prefetch=1,
            grid=(8,),
            in_specs=[
                whole(256, 1024),
                whole(256, 1024),
                pl.BlockSpec((512, 256), lambda i, pos: (0, (pos[2] ^ i) * 2 + pos[0])),
                pl.BlockSpec((512, 256), lambda i, pos: (0, pos[2] ^ i)),
            ],
            out_specs=[whole(2, 2, 256, 256)] * 3 + [whole(2, 256, 256)] * 2,
        ),
        out_shape=[shape((2, 2, 256, 256))] * 3 + [shape((2, 256, 256))] * 2,
        compiler_params=params(),
        cost_estimate=cost(5.0),
        name="weight_term",
    )(pos, attn, attn_other, output_grad, grad_recv)


def grad_block(key, value, qt, da, row_dot, s, e_ref, slot, ds_ref, dq_ref, first):
    da_low = (da * s).astype(BF)
    dot_scaled = row_dot * s
    for c in range(NQ):
        cols = slice(c * QC, (c + 1) * QC)
        dp = mm(value, da_low[:, cols], NN)
        ds = (e_ref[0, slot, :, cols].astype(F32) * (dp - dot_scaled[:, cols])).astype(BF)
        ds_ref[:, cols] = ds
        part = mm(key, ds, TN)
        if first:
            dq_ref[:, cols] = part
        else:
            dq_ref[:, cols] += part
    dk = mm(ds_ref[...], qt, NT) * SCALE
    dv = mm(e_ref[0, slot], da_low, NT)
    return dk, dv


def grad_rows(da_own, da_recv, o_ref):
    da = jnp.concatenate([da_own[...], da_recv[...]], axis=1).astype(F32)
    return da, jnp.sum(da * o_ref[...].astype(F32), axis=0, keepdims=True)


def far_grad_kernel(qt_ref, da_own, da_recv, o_ref, s_ref, e_middle, e_last, *refs):
    keys, values = refs[:3], refs[3:6]
    side_ref, z1_ref, z3_ref, z2_ref, dq_ref, ds_ref = refs[6:]
    head = pl.program_id(0)
    da, row_dot = grad_rows(da_own, da_recv, o_ref)
    k_cols = pl.ds(pl.multiple_of(head * 128, 128), 128)
    v_cols = pl.ds(pl.multiple_of(head * 128 + 256, 128), 128)
    qt = qt_ref[...]
    for j in range(3):
        s = s_ref[0, 2 + j : 3 + j, :]
        both = grad_block(
            keys[j][...],
            values[j][...],
            qt,
            da,
            row_dot,
            s,
            e_last if j == 2 else e_middle,
            j % 2,
            ds_ref,
            dq_ref,
            j == 0,
        )
        for cols, grad in zip((k_cols, v_cols), both):
            grad = grad.astype(BF)
            if j == 0:
                side_ref[:, cols] = grad
            else:
                at = j - 1
                z1_ref[at * 256 : at * 256 + 256, cols] = grad[:256]
                z3_ref[at * 128 : at * 128 + 128, cols] = grad[256:384]
                z2_ref[at * 128 : at * 128 + 128, cols] = grad[384:]


def common_specs():
    return [
        pl.BlockSpec((128, 1024), lambda h: (h, 0)),
        pl.BlockSpec((128, 512), lambda h: (h, 0)),
        pl.BlockSpec((128, 512), lambda h: (h, 0)),
        pl.BlockSpec((128, 1024), lambda h: (h, 0)),
        pl.BlockSpec((1, 8, 1024), lambda h: (h, 0, 0)),
    ]


def far_grad_call(qt, da_own, da_recv, attn, scales, e_middle, e_last, far):
    return pl.pallas_call(
        far_grad_kernel,
        grid=(2,),
        in_specs=[
            *common_specs(),
            per_head(1, 2, 512, 1024),
            per_head(1, 1, 512, 1024),
            *kv_specs(3),
        ],
        out_specs=[pl.BlockSpec((rows, 512), lambda h: (0, 0)) for rows in (512, 512, 256, 256)]
        + [pl.BlockSpec((128, 1024), lambda h: (h, 0))],
        out_shape=[shape((rows, 512)) for rows in (512, 512, 256, 256)] + [shape((256, 1024), F32)],
        scratch_shapes=[pltpu.VMEM((512, 1024), BF)],
        compiler_params=params(),
        cost_estimate=cost(6.7),
        name="far_grads",
    )(qt, da_own, da_recv, attn, scales, e_middle, e_last, *far, *far)


def near_grad_kernel(
    qt_ref,
    da_own,
    da_recv,
    o_ref,
    s_ref,
    e_ref,
    k_own,
    k_sib,
    v_own,
    v_sib,
    dq_in,
    kv_ref,
    q_own,
    q_send,
    ds_ref,
    dq_ref,
):
    keys, values = (k_own, k_sib), (v_own, v_sib)
    head = pl.program_id(0)
    da, row_dot = grad_rows(da_own, da_recv, o_ref)
    k_cols = pl.ds(pl.multiple_of(head * 128, 128), 128)
    v_cols = pl.ds(pl.multiple_of(head * 128 + 256, 128), 128)
    qt = qt_ref[...]
    dq_ref[...] = dq_in[...]
    for j in range(2):
        rows = slice(j * 512, (j + 1) * 512)
        s = s_ref[0, j : j + 1, :]
        dk, dv = grad_block(
            keys[j][...], values[j][...], qt, da, row_dot, s, e_ref, j, ds_ref, dq_ref, False
        )
        kv_ref[rows, k_cols] = dk
        kv_ref[rows, v_cols] = dv
    q_own[...] = (dq_ref[:, :512] * SCALE).T.astype(BF)
    q_send[...] = (dq_ref[:, 512:] * SCALE).T.astype(BF)


def near_grad_call(qt, da_own, da_recv, attn, scales, e_near, own, sib, dq):
    return pl.pallas_call(
        near_grad_kernel,
        grid=(2,),
        in_specs=[
            *common_specs(),
            pl.BlockSpec((1, 2, 512, 1024), lambda h: (h, 0, 0, 0)),
            *kv_specs(2),
            pl.BlockSpec((128, 1024), lambda h: (h, 0)),
        ],
        out_specs=[
            pl.BlockSpec((1024, 512), lambda h: (0, 0)),
            pl.BlockSpec((512, 128), lambda h: (0, h)),
            pl.BlockSpec((512, 128), lambda h: (0, h)),
        ],
        out_shape=[shape((1024, 512), F32), shape((512, 256)), shape((512, 256))],
        scratch_shapes=[pltpu.VMEM((512, 1024), BF), pltpu.VMEM((128, 1024), F32)],
        compiler_params=params(),
        cost_estimate=cost(4.8),
        name="near_grads",
    )(qt, da_own, da_recv, attn, scales, e_near, own, sib, own, sib, dq)


def spread(rows, level, refs, part):
    n = rows >> level
    wide = band(rows, n, 1 << level, 0.5**level, False)
    return [mm(wide, ref[part * n : (part + 1) * n, :], NN) for ref in refs]


def relay_kernel(side_ref, z1_ref, z3_ref, z2_ref, out_ref):
    parts = spread(512, 1, [z1_ref], 1) + spread(512, 2, [z3_ref, z2_ref], 1)
    out_ref[...] = functools.reduce(jnp.add, parts, side_ref[...].astype(F32)).astype(BF)


def relay_call(side, *along):
    return pl.pallas_call(
        relay_kernel,
        out_shape=shape((512, 512)),
        compiler_params=params(),
        cost_estimate=cost(0.6),
        name="relay",
    )(side, *along)


def collect_kernel(kv_ref, q_ref, side_ref, z1_ref, z3_ref, z2_ref, own_ref, send_ref):
    send_ref[:, 512:] = q_ref[...]
    for part, out in ((1, send_ref), (0, own_ref)):
        total = kv_ref[part * 512 : (part + 1) * 512, :]
        parts = spread(512, 1, [side_ref], part)
        parts += spread(512, 2, [z1_ref.at[:256]], part)
        parts += spread(512, 3, [z3_ref.at[:128], z2_ref.at[:128]], part)
        out[:, :512] = functools.reduce(jnp.add, parts, total).astype(BF)


def collect_call(kv_grad, q_send, side, *along):
    return pl.pallas_call(
        collect_kernel,
        out_shape=[shape((512, 512)), shape((512, 768))],
        compiler_params=params(),
        cost_estimate=cost(1.3),
        name="collect",
    )(kv_grad, q_send, side, *along)


def place_kernel(pos, q_own, kv_own, recv, q_out, k_out, v_out):
    mine = pl.ds(pl.multiple_of(pos[0] * 256, 256), 256)
    other = pl.ds(pl.multiple_of((1 - pos[0]) * 256, 256), 256)
    q_out[:, mine] = q_own[...]
    q_out[:, other] = recv[:, 512:]
    k_out[:, mine] = kv_own[:, :256]
    k_out[:, other] = recv[:, :256]
    v_out[:, mine] = kv_own[:, 256:]
    v_out[:, other] = recv[:, 256:512]


def place_call(pos, q_own, kv_own, recv):
    return pl.pallas_call(
        place_kernel,
        grid_spec=pltpu.PrefetchScalarGridSpec(
            num_scalar_prefetch=1,
            grid=(1,),
            in_specs=[whole(512, 256), whole(512, 512), whole(512, 768)],
            out_specs=[whole(512, 512)] * 3,
        ),
        out_shape=[shape((512, 512))] * 3,
        compiler_params=params(),
        cost_estimate=cost(1.0),
        name="place",
    )(pos, q_own, kv_own, recv)


def total(*terms):
    return functools.reduce(jnp.add, [t.astype(F32) for t in terms])


def cross_kernel(keep, c1, c3, o1, o3, out_ref):
    out_ref[:256, :] = total(keep[:256, :], c1[256:, :], o3[:256, :]).astype(BF)
    out_ref[256:, :] = total(keep[256:, :], c3[256:, :], o1[:256, :]).astype(BF)


def output_kernel(keep, o1, o3, end_1, end_3, cross, out_ref):
    out_ref[:256, :] = total(keep[:256, :], o1[512:, :], end_3[...], cross[:256, :]).astype(BF)
    out_ref[256:, :] = total(keep[256:, :], o3[512:, :], end_1[...], cross[256:, :]).astype(BF)


def weight_sum_kernel(keep, w1, w3, end_1, end_3, own_ref, send_ref):
    up = total(keep[0], w1[1], end_3[...])
    down = total(keep[1], w3[1], end_1[...])
    own_ref[0] = up[0]
    own_ref[1] = down[0]
    send_ref[0] = up[1].astype(BF)
    send_ref[1] = down[1].astype(BF)


def weight_out_kernel(pos, own, back, out_ref):
    for part in range(2):
        row = pos[0] * 256 if part == 0 else (1 - pos[0]) * 256
        rows = pl.ds(pl.multiple_of(row, 256), 256)
        out_ref[rows, :] = total(own[part], back[part]).astype(BF)


def plain_call(kernel, out_shape, us, name, *args):
    return pl.pallas_call(
        kernel,
        out_shape=out_shape,
        compiler_params=params(),
        cost_estimate=cost(us),
        name=name,
    )(*args)


def weight_out_call(pos, own, back):
    return pl.pallas_call(
        weight_out_kernel,
        grid_spec=pltpu.PrefetchScalarGridSpec(
            num_scalar_prefetch=1,
            grid=(1,),
            in_specs=[whole(2, 256, 256)] * 2,
            out_specs=whole(512, 256),
        ),
        out_shape=shape((512, 256)),
        compiler_params=params(),
        cost_estimate=cost(1.0),
        name="weight_out",
    )(pos, own, back)


def add(*terms):
    return functools.reduce(jnp.add, [t.astype(F32) for t in terms])


def after(values, *done):
    return lax.optimization_barrier((values, done))[0]


def low(*terms):
    return add(*terms).astype(BF)


def shards(queries, key_rows, value_rows, out_weight, output_grad):
    ctx = lax.axis_index("ctx")
    core = ctx % 2
    pos = jnp.stack([core, lax.axis_index("head"), ctx // 2]).astype(jnp.int32)

    k_recv, v_recv, q_recv = [swap(a, "ctx", 1) for a in (key_rows, value_rows, queries)]
    qt_own, kv_own, l1_own = prepare_call(pos, queries, key_rows, value_rows)
    k_recv, v_recv = after((k_recv, v_recv), q_recv)
    kv_sib, l1 = pool_call(pos, k_recv, v_recv, l1_own)
    side = swap(l1, "ctx", 2)
    l2, l3, qt = pool_more_call(pos, l1, qt_own, q_recv)
    along = [swap(a, "ctx", mask) for a, mask in ((l2, 4), (l3, 12), (l3, 8))]
    e_near, *carry = score_call(near_kernel, "near_scores", 4.2, qt, (kv_own, kv_sib), ())
    level = after(jnp.concatenate(along, axis=0), e_near, side)
    cross_level = swap(level, "ctx", 2)
    e_middle, *carry = score_call(
        middle_kernel, "middle_scores", 4.2, qt, (side, level), carry
    )
    da_own, da_send, grad_send = grad_attention_call(
        pos, *after((out_weight, output_grad), level)
    )
    cross_level = after(cross_level, da_own, e_middle)
    da_recv, grad_recv = [swap(a, "ctx", 1) for a in after((da_send, grad_send), cross_level)]
    e_last, attn, scales = score_call(
        last_kernel, "last_scores", 2.2, qt, (cross_level,), carry, True
    )
    far = (side, level, cross_level)

    attn_other = after(swap(attn, "ctx", 1), da_recv, grad_recv)
    keep_c, first_c1, first_c3, late_c1, late_c3 = project_call(
        pos, attn, attn_other, out_weight, 1
    )
    got_c1, got_c3 = swap(first_c1, "head", 2), swap(first_c3, "head", 6)

    attn_g, qt_g = after((attn, qt), keep_c)
    side_grad, *level_grads, dq = far_grad_call(
        qt_g, da_own, da_recv, attn_g, scales, e_middle, e_last, far
    )
    back = [swap(g, "ctx", mask) for g, mask in zip(level_grads, (4, 12, 8))]

    attn_p, other_p = after((attn, attn_other), side_grad)
    keep_o, first_o1, first_o3, late_o1, late_o3 = project_call(
        pos, attn_p, other_p, out_weight, 0
    )
    attn_w, other_w = after((attn, attn_other), keep_o)
    keep_w, first_w1, first_w3, late_w1, late_w3 = weight_call(
        pos, attn_w, other_w, output_grad, grad_recv
    )
    qt_n, da_n = after((qt, da_own), keep_w)
    kv_grad, q_own, q_send = near_grad_call(qt_n, da_n, da_recv, attn, scales, e_near, kv_own, kv_sib, dq)

    send_1 = jnp.concatenate([low(late_c1, got_c3[:256]), first_o1], axis=0)
    send_3 = jnp.concatenate([low(late_c3, got_c1[:256]), first_o3], axis=0)
    send_1, send_3 = after((send_1, send_3))
    got_o1, got_o3 = swap(send_1, "head", 2), swap(send_3, "head", 6)

    relayed = relay_call(after(side_grad, send_1, send_3, kv_grad), *back)
    side_back = swap(relayed, "ctx", 2)
    first_w1, first_w3 = after((first_w1, first_w3), back[1:])
    got_w1, got_w3 = swap(first_w1, "ctx", 4), swap(first_w3, "ctx", 12)

    cross = plain_call(
        cross_kernel, shape((512, 512)), 1.0, "cross", keep_c, got_c1, got_c3, got_o1, got_o3
    )
    got_w1, got_w3 = after((got_w1, got_w3), relayed)
    cross_back = swap(cross, "head", 1)
    end_1 = swap(low(late_o1, got_o3[256:512]), "head", 2)
    end_3 = swap(low(late_o3, got_o1[256:512]), "head", 6)
    layer_output = plain_call(
        output_kernel, shape((512, 512)), 1.0, "output", keep_o, got_o1, got_o3, end_1, end_3, cross_back
    )

    end_w1 = swap(low(late_w1, got_w3[0]), "ctx", 4)
    end_w3 = swap(low(late_w3, got_w1[0]), "ctx", 12)
    w_own, w_send = plain_call(
        weight_sum_kernel,
        [shape((2, 256, 256), F32), shape((2, 256, 256))],
        1.0,
        "weight_sum",
        *(after(keep_w, cross), got_w1, got_w3, end_w1, end_w3),
    )
    weight_grad = weight_out_call(pos, w_own, swap(w_send, "ctx", 2))

    kv_done, send = collect_call(after(kv_grad, got_w1), q_send, side_back, *back)
    query_grad, key_grad, value_grad = place_call(pos, q_own, kv_done, swap(send, "ctx", 1))
    return (layer_output, query_grad, key_grad, value_grad, weight_grad)


def solution(mesh):
    placed = (P("ctx", "head"), P("ctx", "head"), P("ctx", "head"), P("head", None), P("ctx", None))
    return jax.shard_map(
        shards,
        mesh=mesh,
        in_specs=placed,
        out_specs=(
            P("ctx", "head"),
            P("ctx", "head"),
            P("ctx", "head"),
            P("ctx", "head"),
            P("head", "ctx"),
        ),
        check_vma=False,
    )
```

```python
import functools
import math

import jax
import jax.numpy as jnp
from jax import lax
from jax.experimental import pallas as pl
from jax.experimental.pallas import tpu as pltpu
from jax.sharding import PartitionSpec as P

HD = 128
BF = jnp.bfloat16
F32 = jnp.float32
SCALE = 1.0 / math.sqrt(HD)
LOG2E = math.log2(math.e)
VMEM_LIMIT = 16 * 1024 * 1024


def cost(us):
    return pl.CostEstimate(flops=0, bytes_accessed=int(us * 1.20e+06), transcendentals=0)


def params(**kw):
    return pltpu.CompilerParams(vmem_limit_bytes=VMEM_LIMIT, **kw)


def mm(a, b, dims):
    return lax.dot_general(a, b, (dims, ((), ())), preferred_element_type=F32)


NN = ((1,), (0,))
NT = ((1,), (1,))
TN = ((0,), (0,))


def swap(value, axis, mask):
    size = lax.axis_size(axis)
    return lax.ppermute(value, axis, [(i, i ^ mask) for i in range(size)])


def shape(dims, dtype=BF):
    return jax.ShapeDtypeStruct(dims, dtype)


def grad_attention_kernel(pos, w_ref, g_ref, keep_ref, send_ref, other_ref, acc):
    step = pl.program_id(0)
    core = pos[0]

    @pl.when(step == 0)
    def _():
        acc[...] = jnp.zeros_like(acc)

    acc[...] += mm(w_ref[...], g_ref[...], NT)
    for part in range(2):
        away = pl.multiple_of((1 - core) * 256 + part * 512, 256)
        other_ref[:, part * 256 : (part + 1) * 256] = g_ref[:, pl.ds(away, 256)]

    @pl.when(step == pl.num_programs(0) - 1)
    def _():
        keep_ref[...] = acc[pl.ds(pl.multiple_of(core * 256, 256), 256), :].astype(BF)
        send_ref[...] = acc[pl.ds(pl.multiple_of((1 - core) * 256, 256), 256), :].astype(BF)


def grad_attention_call(pos, out_weight, output_grad):
    width = output_grad.shape[1]
    step = 1024
    return pl.pallas_call(
        grad_attention_kernel,
        grid_spec=pltpu.PrefetchScalarGridSpec(
            num_scalar_prefetch=1,
            grid=(width // step,),
            in_specs=[
                pl.BlockSpec((512, step), lambda i, pos: (0, i)),
                pl.BlockSpec((512, step), lambda i, pos: (0, i)),
            ],
            out_specs=[
                pl.BlockSpec((256, 512), lambda i, pos: (0, 0)),
                pl.BlockSpec((256, 512), lambda i, pos: (0, 0)),
                pl.BlockSpec((512, step // 2), lambda i, pos: (0, i)),
            ],
            scratch_shapes=[pltpu.VMEM((512, 512), F32)],
        ),
        out_shape=[shape((256, 512)), shape((256, 512)), shape((512, width // 2))],
        compiler_params=params(),
        cost_estimate=cost(4.5),
        name="grad_attention",
    )(pos, out_weight, output_grad)


def band(rows, cols, ratio, weight, row_major):
    r = lax.broadcasted_iota(jnp.int32, (rows, cols), 0)
    c = lax.broadcasted_iota(jnp.int32, (rows, cols), 1)
    hit = (c // ratio == r) if row_major else (r // ratio == c)
    return jnp.where(hit, weight, 0.0).astype(BF)


def prepare_kernel(pos, q_ref, k_ref, v_ref, qt_ref, kv_ref, l1_ref):
    fold = band(256, 512, 2, 0.5, True)
    for at, ref in enumerate((k_ref, v_ref)):
        cols = slice(at * 256, (at + 1) * 256)
        kv_ref[:, cols] = ref[...]
        l1_ref[:, cols] = mm(fold, ref[...], NN).astype(BF)
    qt_ref[...] = q_ref[...].T


def pool_kernel(pos, k_ref, v_ref, own_ref, kv_ref, l1_ref):
    fold = band(256, 512, 2, 0.5, True)
    l1_ref[:256, :] = own_ref[...]
    for at, ref in enumerate((k_ref, v_ref)):
        cols = slice(at * 256, (at + 1) * 256)
        kv_ref[:, cols] = ref[...]
        l1_ref[256:, cols] = mm(fold, ref[...], NN).astype(BF)


def whole(*dims):
    return pl.BlockSpec(dims, lambda i, pos: (0,) * len(dims))


def half_cols():
    return pl.BlockSpec((512, 256), lambda i, pos: (0, pos[0]))


def prepare_call(pos, queries, keys, values):
    return pl.pallas_call(
        prepare_kernel,
        grid_spec=pltpu.PrefetchScalarGridSpec(
            num_scalar_prefetch=1,
            grid=(1,),
            in_specs=[half_cols()] * 3,
            out_specs=[whole(256, 512), whole(512, 512), whole(256, 512)],
        ),
        out_shape=[shape((256, 512)), shape((512, 512)), shape((256, 512))],
        compiler_params=params(),
        cost_estimate=cost(1.0),
        name="prepare",
    )(pos, queries, keys, values)


def pool_call(pos, keys, values, l1_own):
    return pl.pallas_call(
        pool_kernel,
        grid_spec=pltpu.PrefetchScalarGridSpec(
            num_scalar_prefetch=1,
            grid=(1,),
            in_specs=[half_cols(), half_cols(), whole(256, 512)],
            out_specs=[whole(512, 512), whole(512, 512)],
        ),
        out_shape=[shape((512, 512)), shape((512, 512))],
        compiler_params=params(),
        cost_estimate=cost(1.0),
        name="pool",
    )(pos, keys, values, l1_own)


def pool_more_kernel(pos, l1_ref, own_ref, q_ref, l2_ref, l3_ref, qt_ref):
    fold = band(256, 512, 2, 0.5, True)
    l2 = mm(fold, l1_ref[...], NN).astype(BF)
    l2_ref[...] = l2
    l3_ref[...] = mm(fold[:128, :256], l2, NN).astype(BF)
    qt_ref[:, :512] = own_ref[...]
    qt_ref[:, 512:] = q_ref[...].T


def pool_more_call(pos, l1, qt_own, queries):
    return pl.pallas_call(
        pool_more_kernel,
        grid_spec=pltpu.PrefetchScalarGridSpec(
            num_scalar_prefetch=1,
            grid=(1,),
            in_specs=[whole(512, 512), whole(256, 512), half_cols()],
            out_specs=[whole(256, 512), whole(128, 512), whole(256, 1024)],
        ),
        out_shape=[shape((256, 512)), shape((128, 512)), shape((256, 1024))],
        compiler_params=params(),
        cost_estimate=cost(1.0),
        name="pool_more",
    )(pos, l1, qt_own, queries)


def score_block(key, value, qt_ref, e_ref, slot, carry):
    new = []
    for c, (m_run, l_run, acc) in enumerate(carry):
        cols = slice(c * QC, (c + 1) * QC)
        s = mm(key, qt_ref[:, cols], NN)
        m = jnp.max(s, axis=0, keepdims=True) * (SCALE * LOG2E)
        e = jnp.exp2(s * (SCALE * LOG2E) - m)
        l = jnp.sum(e, axis=0, keepdims=True)
        e_low = e.astype(BF)
        e_ref[0, slot, :, cols] = e_low
        u = mm(value, e_low, TN)
        if m_run is None:
            new.append((m, l, u, m))
        else:
            top = jnp.maximum(m_run, m)
            f_run, f_new = jnp.exp2(m_run - top), jnp.exp2(m - top)
            new.append((top, l_run * f_run + l * f_new, acc * f_run + u * f_new, m))
    return new


QC = 1024
NQ = 1


def near_kernel(qt_ref, *refs):
    keys, values = refs[:2], refs[2:4]
    e_ref, acc_ref, st_ref = refs[4:]
    carry = [(None, None, None)] * NQ
    for j in range(2):
        got = score_block(keys[j][...], values[j][...], qt_ref, e_ref, j, carry)
        carry = [g[:3] for g in got]
        for c in range(NQ):
            st_ref[0, 2 + j : 3 + j, c * QC : (c + 1) * QC] = got[c][3]
    put_carry(carry, acc_ref, st_ref)


def put_carry(carry, acc_ref, st_ref):
    for c, (m, l, acc) in enumerate(carry):
        cols = slice(c * QC, (c + 1) * QC)
        acc_ref[:, cols] = acc
        st_ref[0, 0:1, cols] = m
        st_ref[0, 1:2, cols] = l


def get_carry(acc_ref, st_ref):
    parts = [slice(c * QC, (c + 1) * QC) for c in range(NQ)]
    return [(st_ref[0, 0:1, p], st_ref[0, 1:2, p], acc_ref[:, p]) for p in parts]


def middle_kernel(qt_ref, *refs):
    keys, values = refs[:2], refs[2:4]
    acc_in, st_in, e_ref, acc_ref, st_ref = refs[4:]
    carry = get_carry(acc_in, st_in)
    st_ref[0, 2:4, :] = st_in[0, 2:4, :]
    for j in range(2):
        got = score_block(keys[j][...], values[j][...], qt_ref, e_ref, j, carry)
        carry = [g[:3] for g in got]
        for c in range(NQ):
            st_ref[0, 4 + j : 5 + j, c * QC : (c + 1) * QC] = got[c][3]
    put_carry(carry, acc_ref, st_ref)


def last_kernel(qt_ref, key, value, acc_in, st_in, e_ref, o_ref, s_ref):
    got = score_block(key[...], value[...], qt_ref, e_ref, 0, get_carry(acc_in, st_in))
    for c, (m, l, acc, top) in enumerate(got):
        cols = slice(c * QC, (c + 1) * QC)
        inv = 1.0 / l
        o_ref[:, cols] = (acc * inv).astype(BF)
        s_ref[0, :4, cols] = jnp.exp2(st_in[0, 2:6, cols] - m) * inv
        s_ref[0, 4:5, cols] = jnp.exp2(top - m) * inv


def per_head(*dims):
    return pl.BlockSpec(dims, lambda h: (h,) + (0,) * (len(dims) - 1))


def kv_specs(count):
    def spec(offset):
        return pl.BlockSpec((512, 128), lambda h: (0, h + offset))

    return [spec(0)] * count + [spec(2)] * count


CARRY_SPECS = [per_head(128, 1024), per_head(1, 8, 1024)]
CARRY = [shape((256, 1024), F32), shape((2, 8, 1024), F32)]


def score_call(kernel, name, us, qt, blocks, carry, last=False):
    n = len(blocks)
    return pl.pallas_call(
        kernel,
        grid=(2,),
        in_specs=[per_head(128, 1024), *kv_specs(n), *CARRY_SPECS[: len(carry)]],
        out_specs=[per_head(1, n, 512, 1024), *CARRY_SPECS],
        out_shape=[
            shape((2, n, 512, 1024)),
            shape((256, 1024)) if last else CARRY[0],
            CARRY[1],
        ],
        compiler_params=params(),
        cost_estimate=cost(us),
        name=name,
    )(qt, *blocks, *blocks, *carry)


def project_kernel(
    pos, o_ref, r_ref, w_mine, w_other, keep, first_1, first_3, late_1, late_3, mine, other
):
    step = pl.program_id(0)

    @pl.when(step == 0)
    def _():
        mine[...] = o_ref[:, :512].T
        other[...] = r_ref[:, 512:].T

    out = (mm(mine[...], w_mine[...], NN) + mm(other[...], w_other[...], NN)).astype(BF)
    top, low = out[:256], out[256:]

    @pl.when(step == 0)
    def _():
        keep[...] = out

    @pl.when(step == 1)
    def _():
        first_1[256:] = top
        late_1[...] = low

    @pl.when(step == 2)
    def _():
        first_1[:256] = top
        first_3[:256] = low

    @pl.when(step == 3)
    def _():
        first_3[256:] = low
        late_3[...] = top


def project_call(pos, attn, attn_other, out_weight, dx):
    def weight(flip):
        return pl.BlockSpec((256, 512), lambda i, pos: (pos[0] ^ flip, pos[1] ^ (i * 2 + dx)))

    return pl.pallas_call(
        project_kernel,
        grid_spec=pltpu.PrefetchScalarGridSpec(
            num_scalar_prefetch=1,
            grid=(4,),
            in_specs=[whole(256, 1024), whole(256, 1024), weight(0), weight(1)],
            out_specs=[whole(512, 512)] * 3 + [whole(256, 512)] * 2,
            scratch_shapes=[pltpu.VMEM((512, 256), BF), pltpu.VMEM((512, 256), BF)],
        ),
        out_shape=[shape((512, 512))] * 3 + [shape((256, 512))] * 2,
        compiler_params=params(),
        cost_estimate=cost(3.0),
        name="project",
    )(pos, attn, attn_other, out_weight, out_weight)


def weight_kernel(pos, o_ref, r_ref, g_own, g_recv, out_ref):
    own, far = g_own[...], g_recv[...]
    out_ref[0, 0] = (mm(o_ref[:, :512], own, NN) + mm(o_ref[:, 512:], far, NN)).astype(BF)
    out_ref[0, 1] = (mm(r_ref[:, 512:], own, NN) + mm(r_ref[:, :512], far, NN)).astype(BF)


def weight_call(pos, attn, attn_other, output_grad, grad_recv, dx):
    return pl.pallas_call(
        weight_kernel,
        grid_spec=pltpu.PrefetchScalarGridSpec(
            num_scalar_prefetch=1,
            grid=(4,),
            in_specs=[
                whole(256, 1024),
                whole(256, 1024),
                pl.BlockSpec((512, 256), lambda i, pos: (0, (pos[2] ^ (2 * i + dx)) * 2 + pos[0])),
                pl.BlockSpec((512, 256), lambda i, pos: (0, pos[2] ^ (2 * i + dx))),
            ],
            out_specs=pl.BlockSpec((1, 2, 256, 256), lambda i, pos: (i, 0, 0, 0)),
        ),
        out_shape=shape((4, 2, 256, 256)),
        compiler_params=params(),
        cost_estimate=cost(2.5),
        name="weight_term",
    )(pos, attn, attn_other, output_grad, grad_recv)


def grad_block(key, value, qt, da, row_dot, s, e_ref, slot, ds_ref, dq_ref, first):
    da_low = (da * s).astype(BF)
    dot_scaled = row_dot * s
    for c in range(NQ):
        cols = slice(c * QC, (c + 1) * QC)
        dp = mm(value, da_low[:, cols], NN)
        ds = (e_ref[0, slot, :, cols].astype(F32) * (dp - dot_scaled[:, cols])).astype(BF)
        ds_ref[:, cols] = ds
        part = mm(key, ds, TN)
        if first:
            dq_ref[:, cols] = part
        else:
            dq_ref[:, cols] += part
    dk = mm(ds_ref[...], qt, NT) * SCALE
    dv = mm(e_ref[0, slot], da_low, NT)
    return dk, dv


def grad_rows(da_own, da_recv, o_ref):
    da = jnp.concatenate([da_own[...], da_recv[...]], axis=1).astype(F32)
    return da, jnp.sum(da * o_ref[...].astype(F32), axis=0, keepdims=True)


def far_grad_kernel(qt_ref, da_own, da_recv, o_ref, s_ref, e_middle, e_last, *refs):
    keys, values = refs[:3], refs[3:6]
    side_ref, z1_ref, z3_ref, z2_ref, dq_ref, ds_ref = refs[6:]
    head = pl.program_id(0)
    da, row_dot = grad_rows(da_own, da_recv, o_ref)
    k_cols = pl.ds(pl.multiple_of(head * 128, 128), 128)
    v_cols = pl.ds(pl.multiple_of(head * 128 + 256, 128), 128)
    qt = qt_ref[...]
    for j in range(3):
        s = s_ref[0, 2 + j : 3 + j, :]
        both = grad_block(
            keys[j][...],
            values[j][...],
            qt,
            da,
            row_dot,
            s,
            e_last if j == 2 else e_middle,
            j % 2,
            ds_ref,
            dq_ref,
            j == 0,
        )
        for cols, grad in zip((k_cols, v_cols), both):
            grad = grad.astype(BF)
            if j == 0:
                side_ref[:, cols] = grad
            else:
                at = j - 1
                z1_ref[at * 256 : at * 256 + 256, cols] = grad[:256]
                z3_ref[at * 128 : at * 128 + 128, cols] = grad[256:384]
                z2_ref[at * 128 : at * 128 + 128, cols] = grad[384:]


def common_specs():
    return [
        pl.BlockSpec((128, 1024), lambda h: (h, 0)),
        pl.BlockSpec((128, 512), lambda h: (h, 0)),
        pl.BlockSpec((128, 512), lambda h: (h, 0)),
        pl.BlockSpec((128, 1024), lambda h: (h, 0)),
        pl.BlockSpec((1, 8, 1024), lambda h: (h, 0, 0)),
    ]


def far_grad_call(qt, da_own, da_recv, attn, scales, e_middle, e_last, far):
    return pl.pallas_call(
        far_grad_kernel,
        grid=(2,),
        in_specs=[
            *common_specs(),
            per_head(1, 2, 512, 1024),
            per_head(1, 1, 512, 1024),
            *kv_specs(3),
        ],
        out_specs=[pl.BlockSpec((rows, 512), lambda h: (0, 0)) for rows in (512, 512, 256, 256)]
        + [pl.BlockSpec((128, 1024), lambda h: (h, 0))],
        out_shape=[shape((rows, 512)) for rows in (512, 512, 256, 256)] + [shape((256, 1024), F32)],
        scratch_shapes=[pltpu.VMEM((512, 1024), BF)],
        compiler_params=params(),
        cost_estimate=cost(6.7),
        name="far_grads",
    )(qt, da_own, da_recv, attn, scales, e_middle, e_last, *far, *far)


def near_grad_kernel(
    qt_ref,
    da_own,
    da_recv,
    o_ref,
    s_ref,
    e_ref,
    k_own,
    k_sib,
    v_own,
    v_sib,
    dq_in,
    kv_ref,
    q_own,
    q_send,
    ds_ref,
    dq_ref,
):
    keys, values = (k_own, k_sib), (v_own, v_sib)
    head = pl.program_id(0)
    da, row_dot = grad_rows(da_own, da_recv, o_ref)
    k_cols = pl.ds(pl.multiple_of(head * 128, 128), 128)
    v_cols = pl.ds(pl.multiple_of(head * 128 + 256, 128), 128)
    qt = qt_ref[...]
    dq_ref[...] = dq_in[...]
    for j in range(2):
        rows = slice(j * 512, (j + 1) * 512)
        s = s_ref[0, j : j + 1, :]
        dk, dv = grad_block(
            keys[j][...], values[j][...], qt, da, row_dot, s, e_ref, j, ds_ref, dq_ref, False
        )
        kv_ref[rows, k_cols] = dk
        kv_ref[rows, v_cols] = dv
    q_own[...] = (dq_ref[:, :512] * SCALE).T.astype(BF)
    q_send[...] = (dq_ref[:, 512:] * SCALE).T.astype(BF)


def near_grad_call(qt, da_own, da_recv, attn, scales, e_near, own, sib, dq):
    return pl.pallas_call(
        near_grad_kernel,
        grid=(2,),
        in_specs=[
            *common_specs(),
            pl.BlockSpec((1, 2, 512, 1024), lambda h: (h, 0, 0, 0)),
            *kv_specs(2),
            pl.BlockSpec((128, 1024), lambda h: (h, 0)),
        ],
        out_specs=[
            pl.BlockSpec((1024, 512), lambda h: (0, 0)),
            pl.BlockSpec((512, 128), lambda h: (0, h)),
            pl.BlockSpec((512, 128), lambda h: (0, h)),
        ],
        out_shape=[shape((1024, 512), F32), shape((512, 256)), shape((512, 256))],
        scratch_shapes=[pltpu.VMEM((512, 1024), BF), pltpu.VMEM((128, 1024), F32)],
        compiler_params=params(),
        cost_estimate=cost(4.8),
        name="near_grads",
    )(qt, da_own, da_recv, attn, scales, e_near, own, sib, own, sib, dq)


def spread(rows, level, refs, part):
    n = rows >> level
    wide = band(rows, n, 1 << level, 0.5**level, False)
    return [mm(wide, ref[part * n : (part + 1) * n, :], NN) for ref in refs]


def relay_kernel(side_ref, z1_ref, z3_ref, z2_ref, out_ref):
    parts = spread(512, 1, [z1_ref], 1) + spread(512, 2, [z3_ref, z2_ref], 1)
    out_ref[...] = functools.reduce(jnp.add, parts, side_ref[...].astype(F32)).astype(BF)


def relay_call(side, *along):
    return pl.pallas_call(
        relay_kernel,
        out_shape=shape((512, 512)),
        compiler_params=params(),
        cost_estimate=cost(0.6),
        name="relay",
    )(side, *along)


def collect_kernel(kv_ref, q_ref, side_ref, z1_ref, z3_ref, z2_ref, own_ref, send_k, send_v):
    send_k[:, 256:] = q_ref[:, :128]
    send_v[:, 256:] = q_ref[:, 128:]
    for part in (1, 0):
        start = kv_ref[part * 512 : (part + 1) * 512, :]
        parts = spread(512, 1, [side_ref], part)
        parts += spread(512, 2, [z1_ref.at[:256]], part)
        parts += spread(512, 3, [z3_ref.at[:128], z2_ref.at[:128]], part)
        done = functools.reduce(jnp.add, parts, start).astype(BF)
        if part:
            send_k[:, :256] = done[:, :256]
            send_v[:, :256] = done[:, 256:]
        else:
            own_ref[...] = done


def collect_call(kv_grad, q_send, side, *along):
    return pl.pallas_call(
        collect_kernel,
        out_shape=[shape((512, 512))] + [shape((512, 384))] * 2,
        compiler_params=params(),
        cost_estimate=cost(1.3),
        name="collect",
    )(kv_grad, q_send, side, *along)


def place_kernel(pos, q_own, kv_own, recv_k, recv_v, q_out, k_out, v_out):
    mine = pl.ds(pl.multiple_of(pos[0] * 256, 256), 256)
    other = pl.ds(pl.multiple_of((1 - pos[0]) * 256, 256), 256)
    q_out[:, mine] = q_own[...]
    base = pl.multiple_of((1 - pos[0]) * 256, 128)
    q_out[:, pl.ds(base, 128)] = recv_k[:, 256:]
    q_out[:, pl.ds(base + 128, 128)] = recv_v[:, 256:]
    k_out[:, mine] = kv_own[:, :256]
    k_out[:, other] = recv_k[:, :256]
    v_out[:, mine] = kv_own[:, 256:]
    v_out[:, other] = recv_v[:, :256]


def place_call(pos, q_own, kv_own, *recv):
    return pl.pallas_call(
        place_kernel,
        grid_spec=pltpu.PrefetchScalarGridSpec(
            num_scalar_prefetch=1,
            grid=(1,),
            in_specs=[whole(512, 256), whole(512, 512)] + [whole(512, 384)] * 2,
            out_specs=[whole(512, 512)] * 3,
        ),
        out_shape=[shape((512, 512))] * 3,
        compiler_params=params(),
        cost_estimate=cost(1.0),
        name="place",
    )(pos, q_own, kv_own, *recv)


def total(*terms):
    return functools.reduce(jnp.add, [t.astype(F32) for t in terms])


def cross_kernel(keep, c1, c3, o1, o3, out_ref):
    out_ref[:256, :] = total(keep[:256, :], c1[256:, :], o3[:256, :]).astype(BF)
    out_ref[256:, :] = total(keep[256:, :], c3[256:, :], o1[:256, :]).astype(BF)


def output_kernel(keep, o1, o3, end_1, end_3, cross, out_ref):
    out_ref[:256, :] = total(keep[:256, :], o1[512:, :], end_3[...], cross[:256, :]).astype(BF)
    out_ref[256:, :] = total(keep[256:, :], o3[512:, :], end_1[...], cross[256:, :]).astype(BF)


def weight_sum_kernel(own, wx, keep, first_1, first_3, late_1, late_3):
    def part(dz, half):
        return total(own[dz, half], wx[dz, half])

    keep[0] = part(0, 0)
    keep[1] = part(0, 1)
    first_1[0] = part(2, 0).astype(BF)
    first_1[1] = part(1, 0).astype(BF)
    first_3[0] = part(2, 1).astype(BF)
    first_3[1] = part(3, 1).astype(BF)
    late_1[...] = part(1, 1).astype(BF)
    late_3[...] = part(3, 0).astype(BF)


def weight_out_kernel(pos, keep, w1, w3, we_1, we_3, out_ref):
    up = total(keep[0], w1[1], we_3[...])
    down = total(keep[1], w3[1], we_1[...])
    for row, part in ((pos[0] * 256, up), ((1 - pos[0]) * 256, down)):
        out_ref[pl.ds(pl.multiple_of(row, 256), 256), :] = part.astype(BF)


def plain_call(kernel, out_shape, us, name, *args):
    return pl.pallas_call(
        kernel,
        out_shape=out_shape,
        compiler_params=params(),
        cost_estimate=cost(us),
        name=name,
    )(*args)


def weight_out_call(pos, *args):
    return pl.pallas_call(
        weight_out_kernel,
        grid_spec=pltpu.PrefetchScalarGridSpec(
            num_scalar_prefetch=1,
            grid=(1,),
            in_specs=[whole(2, 256, 256)] * 3 + [whole(256, 256)] * 2,
            out_specs=whole(512, 256),
        ),
        out_shape=shape((512, 256)),
        compiler_params=params(),
        cost_estimate=cost(1.0),
        name="weight_out",
    )(pos, *args)


def add(*terms):
    return functools.reduce(jnp.add, [t.astype(F32) for t in terms])


def after(values, *done):
    return lax.optimization_barrier((values, done))[0]


def low(*terms):
    return add(*terms).astype(BF)


def shards(queries, key_rows, value_rows, out_weight, output_grad):
    ctx = lax.axis_index("ctx")
    core = ctx % 2
    pos = jnp.stack([core, lax.axis_index("head"), ctx // 2]).astype(jnp.int32)

    k_recv, v_recv, q_recv = [swap(a, "ctx", 1) for a in (key_rows, value_rows, queries)]
    qt_own, kv_own, l1_own = prepare_call(pos, queries, key_rows, value_rows)
    k_recv, v_recv = after((k_recv, v_recv), q_recv)
    kv_sib, l1 = pool_call(pos, k_recv, v_recv, l1_own)
    side = swap(l1, "ctx", 2)
    l2, l3, qt = pool_more_call(pos, l1, qt_own, q_recv)
    along = [swap(a, "ctx", mask) for a, mask in ((l2, 4), (l3, 12), (l3, 8))]
    e_near, *carry = score_call(near_kernel, "near_scores", 4.2, qt, (kv_own, kv_sib), ())
    level = after(jnp.concatenate(along, axis=0), e_near, side)
    cross_level = swap(level, "ctx", 2)
    e_middle, *carry = score_call(
        middle_kernel, "middle_scores", 4.2, qt, (side, level), carry
    )
    da_own, da_send, grad_send = grad_attention_call(
        pos, *after((out_weight, output_grad), level)
    )
    cross_level = after(cross_level, da_own, e_middle)
    da_recv, grad_recv = [swap(a, "ctx", 1) for a in after((da_send, grad_send), cross_level)]
    e_last, attn, scales = score_call(
        last_kernel, "last_scores", 2.2, qt, (cross_level,), carry, True
    )
    far = (side, level, cross_level)

    attn_other = after(swap(attn, "ctx", 1), da_recv, grad_recv)
    keep_c, first_c1, first_c3, late_c1, late_c3 = project_call(
        pos, attn, attn_other, out_weight, 1
    )
    got_c1, got_c3 = swap(first_c1, "head", 2), swap(first_c3, "head", 6)

    attn_v, other_v = after((attn, attn_other), keep_c)
    w_cross = weight_call(pos, attn_v, other_v, output_grad, grad_recv, 1)
    w_recv = swap(w_cross, "ctx", 2)

    attn_g, qt_g = after((attn, qt), w_cross)
    side_grad, *level_grads, dq = far_grad_call(
        qt_g, da_own, da_recv, attn_g, scales, e_middle, e_last, far
    )
    back = [swap(g, "ctx", mask) for g, mask in zip(level_grads[:2], (4, 12))]

    attn_p, other_p = after((attn, attn_other), side_grad)
    keep_o, first_o1, first_o3, late_o1, late_o3 = project_call(
        pos, attn_p, other_p, out_weight, 0
    )
    send_1 = jnp.concatenate([low(late_c1, got_c3[:256]), first_o1], axis=0)
    send_3 = jnp.concatenate([low(late_c3, got_c1[:256]), first_o3], axis=0)
    send_1, send_3 = after((send_1, send_3))
    got_o1, got_o3 = swap(send_1, "head", 2), swap(send_3, "head", 6)
    back.append(swap(after(level_grads[2], back[1]), "ctx", 8))
    attn_w, other_w = after((attn, attn_other), (keep_o, send_1, send_3))
    w_own = weight_call(pos, attn_w, other_w, output_grad, grad_recv, 0)
    qt_n, da_n = after((qt, da_own), w_own)
    kv_grad, q_own, q_send = near_grad_call(
        qt_n, da_n, da_recv, attn, scales, e_near, kv_own, kv_sib, dq
    )

    relayed = relay_call(after(side_grad, send_1, send_3, kv_grad), *back)
    side_back = swap(relayed, "ctx", 2)
    keep_w, first_w1, first_w3, late_w1, late_w3 = plain_call(
        weight_sum_kernel,
        [shape((2, 256, 256), F32)] + [shape((2, 256, 256))] * 2 + [shape((256, 256))] * 2,
        0.5,
        "weight_sum",
        *(after(w_own, relayed), w_recv),
    )
    got_w1, got_w3 = swap(first_w1, "ctx", 4), swap(first_w3, "ctx", 12)

    cross = plain_call(
        cross_kernel, shape((512, 512)), 1.0, "cross", keep_c, got_c1, got_c3, got_o1, got_o3
    )
    got_w1, got_w3 = after((got_w1, got_w3), (relayed, cross))
    cross_back = swap(cross, "head", 1)
    end_1 = swap(low(late_o1, got_o3[256:512]), "head", 2)
    end_3 = swap(low(late_o3, got_o1[256:512]), "head", 6)
    end_w1 = swap(low(late_w1, got_w3[0]), "ctx", 4)
    end_w3 = swap(low(late_w3, got_w1[0]), "ctx", 12)
    weight_grad = weight_out_call(pos, keep_w, got_w1, got_w3, end_w1, end_w3)

    layer_output = plain_call(
        output_kernel, shape((512, 512)), 1.0, "output", keep_o, got_o1, got_o3, end_1, end_3, cross_back
    )
    kv_done, *sends = collect_call(after(kv_grad, (end_w1, end_w3)), q_send, side_back, *back)
    query_grad, key_grad, value_grad = place_call(pos, q_own, kv_done, *[swap(a, "ctx", 1) for a in sends])
    return (layer_output, query_grad, key_grad, value_grad, weight_grad)


def solution(mesh):
    placed = (P("ctx", "head"), P("ctx", "head"), P("ctx", "head"), P("head", None), P("ctx", None))
    return jax.shard_map(
        shards,
        mesh=mesh,
        in_specs=placed,
        out_specs=(
            P("ctx", "head"),
            P("ctx", "head"),
            P("ctx", "head"),
            P("ctx", "head"),
            P("head", "ctx"),
        ),
        check_vma=False,
    )
```

```python
import functools
import math

import jax
import jax.numpy as jnp
from jax import lax
from jax.experimental import pallas as pl
from jax.experimental.pallas import tpu as pltpu
from jax.sharding import PartitionSpec as P

HD = 128
BF = jnp.bfloat16
F32 = jnp.float32
SCALE = 1.0 / math.sqrt(HD)
LOG2E = math.log2(math.e)
VMEM_LIMIT = 16 * 1024 * 1024


def cost(us):
    return pl.CostEstimate(flops=0, bytes_accessed=int(us * 1.20e+06), transcendentals=0)


def params(**kw):
    return pltpu.CompilerParams(vmem_limit_bytes=VMEM_LIMIT, **kw)


def mm(a, b, dims):
    return lax.dot_general(a, b, (dims, ((), ())), preferred_element_type=F32)


NN = ((1,), (0,))
NT = ((1,), (1,))
TN = ((0,), (0,))


def swap(value, axis, mask):
    size = lax.axis_size(axis)
    return lax.ppermute(value, axis, [(i, i ^ mask) for i in range(size)])


def shape(dims, dtype=BF):
    return jax.ShapeDtypeStruct(dims, dtype)


def grad_attention_kernel(pos, w_ref, g_ref, keep_ref, send_ref, other_ref, acc):
    step = pl.program_id(0)
    core = pos[0]

    @pl.when(step == 0)
    def _():
        acc[...] = jnp.zeros_like(acc)

    acc[...] += mm(w_ref[...], g_ref[...], NT)
    for part in range(2):
        away = pl.multiple_of((1 - core) * 256 + part * 512, 256)
        other_ref[:, part * 256 : (part + 1) * 256] = g_ref[:, pl.ds(away, 256)]

    @pl.when(step == pl.num_programs(0) - 1)
    def _():
        keep_ref[...] = acc[pl.ds(pl.multiple_of(core * 256, 256), 256), :].astype(BF)
        send_ref[...] = acc[pl.ds(pl.multiple_of((1 - core) * 256, 256), 256), :].astype(BF)


def grad_attention_call(pos, out_weight, output_grad):
    width = output_grad.shape[1]
    step = 1024
    return pl.pallas_call(
        grad_attention_kernel,
        grid_spec=pltpu.PrefetchScalarGridSpec(
            num_scalar_prefetch=1,
            grid=(width // step,),
            in_specs=[
                pl.BlockSpec((512, step), lambda i, pos: (0, i)),
                pl.BlockSpec((512, step), lambda i, pos: (0, i)),
            ],
            out_specs=[
                pl.BlockSpec((256, 512), lambda i, pos: (0, 0)),
                pl.BlockSpec((256, 512), lambda i, pos: (0, 0)),
                pl.BlockSpec((512, step // 2), lambda i, pos: (0, i)),
            ],
            scratch_shapes=[pltpu.VMEM((512, 512), F32)],
        ),
        out_shape=[shape((256, 512)), shape((256, 512)), shape((512, width // 2))],
        compiler_params=params(),
        cost_estimate=cost(4.5),
        name="grad_attention",
    )(pos, out_weight, output_grad)


def band(rows, cols, ratio, weight, row_major):
    r = lax.broadcasted_iota(jnp.int32, (rows, cols), 0)
    c = lax.broadcasted_iota(jnp.int32, (rows, cols), 1)
    hit = (c // ratio == r) if row_major else (r // ratio == c)
    return jnp.where(hit, weight, 0.0).astype(BF)


def prepare_kernel(pos, q_ref, k_ref, v_ref, qt_ref, kv_ref, l1_ref):
    fold = band(256, 512, 2, 0.5, True)
    for at, ref in enumerate((k_ref, v_ref)):
        cols = slice(at * 256, (at + 1) * 256)
        kv_ref[:, cols] = ref[...]
        l1_ref[:, cols] = mm(fold, ref[...], NN).astype(BF)
    qt_ref[...] = q_ref[...].T


def pool_kernel(pos, k_ref, v_ref, own_ref, kv_ref, l1_ref):
    fold = band(256, 512, 2, 0.5, True)
    l1_ref[:256, :] = own_ref[...]
    for at, ref in enumerate((k_ref, v_ref)):
        cols = slice(at * 256, (at + 1) * 256)
        kv_ref[:, cols] = ref[...]
        l1_ref[256:, cols] = mm(fold, ref[...], NN).astype(BF)


def whole(*dims):
    return pl.BlockSpec(dims, lambda i, pos: (0,) * len(dims))


def half_cols():
    return pl.BlockSpec((512, 256), lambda i, pos: (0, pos[0]))


def prepare_call(pos, queries, keys, values):
    return pl.pallas_call(
        prepare_kernel,
        grid_spec=pltpu.PrefetchScalarGridSpec(
            num_scalar_prefetch=1,
            grid=(1,),
            in_specs=[half_cols()] * 3,
            out_specs=[whole(256, 512), whole(512, 512), whole(256, 512)],
        ),
        out_shape=[shape((256, 512)), shape((512, 512)), shape((256, 512))],
        compiler_params=params(),
        cost_estimate=cost(1.0),
        name="prepare",
    )(pos, queries, keys, values)


def pool_call(pos, keys, values, l1_own):
    return pl.pallas_call(
        pool_kernel,
        grid_spec=pltpu.PrefetchScalarGridSpec(
            num_scalar_prefetch=1,
            grid=(1,),
            in_specs=[half_cols(), half_cols(), whole(256, 512)],
            out_specs=[whole(512, 512), whole(512, 512)],
        ),
        out_shape=[shape((512, 512)), shape((512, 512))],
        compiler_params=params(),
        cost_estimate=cost(1.0),
        name="pool",
    )(pos, keys, values, l1_own)


def pool_more_kernel(pos, l1_ref, own_ref, q_ref, l2_ref, l3_ref, qt_ref):
    fold = band(256, 512, 2, 0.5, True)
    l2 = mm(fold, l1_ref[...], NN).astype(BF)
    l2_ref[...] = l2
    l3_ref[...] = mm(fold[:128, :256], l2, NN).astype(BF)
    qt_ref[:, :512] = own_ref[...]
    qt_ref[:, 512:] = q_ref[...].T


def pool_more_call(pos, l1, qt_own, queries):
    return pl.pallas_call(
        pool_more_kernel,
        grid_spec=pltpu.PrefetchScalarGridSpec(
            num_scalar_prefetch=1,
            grid=(1,),
            in_specs=[whole(512, 512), whole(256, 512), half_cols()],
            out_specs=[whole(256, 512), whole(128, 512), whole(256, 1024)],
        ),
        out_shape=[shape((256, 512)), shape((128, 512)), shape((256, 1024))],
        compiler_params=params(),
        cost_estimate=cost(1.0),
        name="pool_more",
    )(pos, l1, qt_own, queries)


def score_block(key, value, qt_ref, e_ref, slot, carry):
    new = []
    for c, (m_run, l_run, acc) in enumerate(carry):
        cols = slice(c * QC, (c + 1) * QC)
        s = mm(key, qt_ref[:, cols], NN)
        m = jnp.max(s, axis=0, keepdims=True) * (SCALE * LOG2E)
        e = jnp.exp2(s * (SCALE * LOG2E) - m)
        l = jnp.sum(e, axis=0, keepdims=True)
        e_low = e.astype(BF)
        e_ref[0, slot, :, cols] = e_low
        u = mm(value, e_low, TN)
        if m_run is None:
            new.append((m, l, u, m))
        else:
            top = jnp.maximum(m_run, m)
            f_run, f_new = jnp.exp2(m_run - top), jnp.exp2(m - top)
            new.append((top, l_run * f_run + l * f_new, acc * f_run + u * f_new, m))
    return new


QC = 1024
NQ = 1


def near_kernel(qt_ref, *refs):
    keys, values = refs[:2], refs[2:4]
    e_ref, acc_ref, st_ref = refs[4:]
    carry = [(None, None, None)] * NQ
    for j in range(2):
        got = score_block(keys[j][...], values[j][...], qt_ref, e_ref, j, carry)
        carry = [g[:3] for g in got]
        for c in range(NQ):
            st_ref[0, 2 + j : 3 + j, c * QC : (c + 1) * QC] = got[c][3]
    put_carry(carry, acc_ref, st_ref)


def put_carry(carry, acc_ref, st_ref):
    for c, (m, l, acc) in enumerate(carry):
        cols = slice(c * QC, (c + 1) * QC)
        acc_ref[:, cols] = acc
        st_ref[0, 0:1, cols] = m
        st_ref[0, 1:2, cols] = l


def get_carry(acc_ref, st_ref):
    parts = [slice(c * QC, (c + 1) * QC) for c in range(NQ)]
    return [(st_ref[0, 0:1, p], st_ref[0, 1:2, p], acc_ref[:, p]) for p in parts]


def middle_kernel(qt_ref, *refs):
    keys, values = refs[:2], refs[2:4]
    acc_in, st_in, e_ref, acc_ref, st_ref = refs[4:]
    carry = get_carry(acc_in, st_in)
    st_ref[0, 2:4, :] = st_in[0, 2:4, :]
    for j in range(2):
        got = score_block(keys[j][...], values[j][...], qt_ref, e_ref, j, carry)
        carry = [g[:3] for g in got]
        for c in range(NQ):
            st_ref[0, 4 + j : 5 + j, c * QC : (c + 1) * QC] = got[c][3]
    put_carry(carry, acc_ref, st_ref)


def last_kernel(qt_ref, key, value, acc_in, st_in, e_ref, o_ref, s_ref):
    got = score_block(key[...], value[...], qt_ref, e_ref, 0, get_carry(acc_in, st_in))
    for c, (m, l, acc, top) in enumerate(got):
        cols = slice(c * QC, (c + 1) * QC)
        inv = 1.0 / l
        o_ref[:, cols] = (acc * inv).astype(BF)
        s_ref[0, :4, cols] = jnp.exp2(st_in[0, 2:6, cols] - m) * inv
        s_ref[0, 4:5, cols] = jnp.exp2(top - m) * inv


def per_head(*dims):
    return pl.BlockSpec(dims, lambda h: (h,) + (0,) * (len(dims) - 1))


def kv_specs(count):
    def spec(offset):
        return pl.BlockSpec((512, 128), lambda h: (0, h + offset))

    return [spec(0)] * count + [spec(2)] * count


CARRY_SPECS = [per_head(128, 1024), per_head(1, 8, 1024)]
CARRY = [shape((256, 1024), F32), shape((2, 8, 1024), F32)]


def score_call(kernel, name, us, qt, blocks, carry, last=False):
    n = len(blocks)
    return pl.pallas_call(
        kernel,
        grid=(2,),
        in_specs=[per_head(128, 1024), *kv_specs(n), *CARRY_SPECS[: len(carry)]],
        out_specs=[per_head(1, n, 512, 1024), *CARRY_SPECS],
        out_shape=[
            shape((2, n, 512, 1024)),
            shape((256, 1024)) if last else CARRY[0],
            CARRY[1],
        ],
        compiler_params=params(),
        cost_estimate=cost(us),
        name=name,
    )(qt, *blocks, *blocks, *carry)


def project_kernel(
    pos, o_ref, r_ref, w_mine, w_other, keep, first_1, first_3, late_1, late_3, mine, other
):
    step = pl.program_id(0)

    @pl.when(step == 0)
    def _():
        mine[...] = o_ref[:, :512].T
        other[...] = r_ref[:, 512:].T

    out = (mm(mine[...], w_mine[...], NN) + mm(other[...], w_other[...], NN)).astype(BF)
    top, low = out[:256], out[256:]

    @pl.when(step == 0)
    def _():
        keep[...] = out

    @pl.when(step == 1)
    def _():
        first_1[256:] = top
        late_1[...] = low

    @pl.when(step == 2)
    def _():
        first_1[:256] = top
        first_3[:256] = low

    @pl.when(step == 3)
    def _():
        first_3[256:] = low
        late_3[...] = top


def project_call(pos, attn, attn_other, out_weight, dx):
    def weight(flip):
        return pl.BlockSpec((256, 512), lambda i, pos: (pos[0] ^ flip, pos[1] ^ (i * 2 + dx)))

    return pl.pallas_call(
        project_kernel,
        grid_spec=pltpu.PrefetchScalarGridSpec(
            num_scalar_prefetch=1,
            grid=(4,),
            in_specs=[whole(256, 1024), whole(256, 1024), weight(0), weight(1)],
            out_specs=[whole(512, 512)] * 3 + [whole(256, 512)] * 2,
            scratch_shapes=[pltpu.VMEM((512, 256), BF), pltpu.VMEM((512, 256), BF)],
        ),
        out_shape=[shape((512, 512))] * 3 + [shape((256, 512))] * 2,
        compiler_params=params(),
        cost_estimate=cost(3.0),
        name="project",
    )(pos, attn, attn_other, out_weight, out_weight)


def project_away_kernel(
    pos, o_ref, r_ref, w_mine, w_other, first_1, first_3, late_1, late_3, mine, other
):
    step = pl.program_id(0) + 1

    @pl.when(step == 1)
    def _():
        mine[...] = o_ref[:, :512].T
        other[...] = r_ref[:, 512:].T

    out = (mm(mine[...], w_mine[...], NN) + mm(other[...], w_other[...], NN)).astype(BF)
    top, low = out[:256], out[256:]

    @pl.when(step == 1)
    def _():
        first_1[256:] = top
        late_1[...] = low

    @pl.when(step == 2)
    def _():
        first_1[:256] = top
        first_3[:256] = low

    @pl.when(step == 3)
    def _():
        first_3[256:] = low
        late_3[...] = top


def project_away_call(pos, attn, attn_other, out_weight, dx):
    def weight(flip):
        return pl.BlockSpec((256, 512), lambda i, pos: (pos[0] ^ flip, pos[1] ^ (i * 2 + 2 + dx)))

    return pl.pallas_call(
        project_away_kernel,
        grid_spec=pltpu.PrefetchScalarGridSpec(
            num_scalar_prefetch=1,
            grid=(3,),
            in_specs=[whole(256, 1024), whole(256, 1024), weight(0), weight(1)],
            out_specs=[whole(512, 512)] * 2 + [whole(256, 512)] * 2,
            scratch_shapes=[pltpu.VMEM((512, 256), BF), pltpu.VMEM((512, 256), BF)],
        ),
        out_shape=[shape((512, 512))] * 2 + [shape((256, 512))] * 2,
        compiler_params=params(),
        cost_estimate=cost(3.0),
        name="project_away",
    )(pos, attn, attn_other, out_weight, out_weight)


def project_keep_kernel(pos, o_ref, r_ref, w_mine, w_other, keep):
    out = mm(o_ref[:, :512], w_mine[...], TN) + mm(r_ref[:, 512:], w_other[...], TN)
    keep[...] = out.astype(BF)


def project_keep_call(pos, attn, attn_other, out_weight, dx):
    def weight(flip):
        return pl.BlockSpec((256, 512), lambda i, pos: (pos[0] ^ flip, pos[1] ^ dx))

    return pl.pallas_call(
        project_keep_kernel,
        grid_spec=pltpu.PrefetchScalarGridSpec(
            num_scalar_prefetch=1,
            grid=(1,),
            in_specs=[whole(256, 1024), whole(256, 1024), weight(0), weight(1)],
            out_specs=whole(512, 512),
        ),
        out_shape=shape((512, 512)),
        compiler_params=params(),
        cost_estimate=cost(1.0),
        name="project_keep",
    )(pos, attn, attn_other, out_weight, out_weight)


def weight_kernel(pos, o_ref, r_ref, g_own, g_recv, out_ref):
    own, far = g_own[...], g_recv[...]
    out_ref[0, 0] = (mm(o_ref[:, :512], own, NN) + mm(o_ref[:, 512:], far, NN)).astype(BF)
    out_ref[0, 1] = (mm(r_ref[:, 512:], own, NN) + mm(r_ref[:, :512], far, NN)).astype(BF)


def weight_call(pos, attn, attn_other, output_grad, grad_recv, dx):
    return pl.pallas_call(
        weight_kernel,
        grid_spec=pltpu.PrefetchScalarGridSpec(
            num_scalar_prefetch=1,
            grid=(4,),
            in_specs=[
                whole(256, 1024),
                whole(256, 1024),
                pl.BlockSpec((512, 256), lambda i, pos: (0, (pos[2] ^ (2 * i + dx)) * 2 + pos[0])),
                pl.BlockSpec((512, 256), lambda i, pos: (0, pos[2] ^ (2 * i + dx))),
            ],
            out_specs=pl.BlockSpec((1, 2, 256, 256), lambda i, pos: (i, 0, 0, 0)),
        ),
        out_shape=shape((4, 2, 256, 256)),
        compiler_params=params(),
        cost_estimate=cost(2.5),
        name="weight_term",
    )(pos, attn, attn_other, output_grad, grad_recv)


def grad_block(key, value, qt, da, row_dot, s, e_ref, slot, ds_ref, dq_ref, first):
    da_low = (da * s).astype(BF)
    dot_scaled = row_dot * s
    for c in range(NQ):
        cols = slice(c * QC, (c + 1) * QC)
        dp = mm(value, da_low[:, cols], NN)
        ds = (e_ref[0, slot, :, cols].astype(F32) * (dp - dot_scaled[:, cols])).astype(BF)
        ds_ref[:, cols] = ds
        part = mm(key, ds, TN)
        if first:
            dq_ref[:, cols] = part
        else:
            dq_ref[:, cols] += part
    dk = mm(ds_ref[...], qt, NT) * SCALE
    dv = mm(e_ref[0, slot], da_low, NT)
    return dk, dv


def grad_rows(da_own, da_recv, o_ref):
    da = jnp.concatenate([da_own[...], da_recv[...]], axis=1).astype(F32)
    return da, jnp.sum(da * o_ref[...].astype(F32), axis=0, keepdims=True)


def far_grad_kernel(qt_ref, da_own, da_recv, o_ref, s_ref, e_middle, e_last, *refs):
    keys, values = refs[:3], refs[3:6]
    side_ref, z1_ref, z3_ref, z2_ref, dq_ref, ds_ref = refs[6:]
    head = pl.program_id(0)
    da, row_dot = grad_rows(da_own, da_recv, o_ref)
    k_cols = pl.ds(pl.multiple_of(head * 128, 128), 128)
    v_cols = pl.ds(pl.multiple_of(head * 128 + 256, 128), 128)
    qt = qt_ref[...]
    for j in range(3):
        s = s_ref[0, 2 + j : 3 + j, :]
        both = grad_block(
            keys[j][...],
            values[j][...],
            qt,
            da,
            row_dot,
            s,
            e_last if j == 2 else e_middle,
            j % 2,
            ds_ref,
            dq_ref,
            j == 0,
        )
        for cols, grad in zip((k_cols, v_cols), both):
            grad = grad.astype(BF)
            if j == 0:
                side_ref[:, cols] = grad
            else:
                at = j - 1
                z1_ref[at * 256 : at * 256 + 256, cols] = grad[:256]
                z3_ref[at * 128 : at * 128 + 128, cols] = grad[256:384]
                z2_ref[at * 128 : at * 128 + 128, cols] = grad[384:]


def common_specs():
    return [
        pl.BlockSpec((128, 1024), lambda h: (h, 0)),
        pl.BlockSpec((128, 512), lambda h: (h, 0)),
        pl.BlockSpec((128, 512), lambda h: (h, 0)),
        pl.BlockSpec((128, 1024), lambda h: (h, 0)),
        pl.BlockSpec((1, 8, 1024), lambda h: (h, 0, 0)),
    ]


def far_grad_call(qt, da_own, da_recv, attn, scales, e_middle, e_last, far):
    return pl.pallas_call(
        far_grad_kernel,
        grid=(2,),
        in_specs=[
            *common_specs(),
            per_head(1, 2, 512, 1024),
            per_head(1, 1, 512, 1024),
            *kv_specs(3),
        ],
        out_specs=[pl.BlockSpec((rows, 512), lambda h: (0, 0)) for rows in (512, 512, 256, 256)]
        + [pl.BlockSpec((128, 1024), lambda h: (h, 0))],
        out_shape=[shape((rows, 512)) for rows in (512, 512, 256, 256)] + [shape((256, 1024), F32)],
        scratch_shapes=[pltpu.VMEM((512, 1024), BF)],
        compiler_params=params(),
        cost_estimate=cost(6.7),
        name="far_grads",
    )(qt, da_own, da_recv, attn, scales, e_middle, e_last, *far, *far)


def near_grad_kernel(
    qt_ref,
    da_own,
    da_recv,
    o_ref,
    s_ref,
    e_ref,
    k_own,
    k_sib,
    v_own,
    v_sib,
    dq_in,
    kv_ref,
    q_own,
    q_send,
    ds_ref,
    dq_ref,
):
    keys, values = (k_own, k_sib), (v_own, v_sib)
    head = pl.program_id(0)
    da, row_dot = grad_rows(da_own, da_recv, o_ref)
    k_cols = pl.ds(pl.multiple_of(head * 128, 128), 128)
    v_cols = pl.ds(pl.multiple_of(head * 128 + 256, 128), 128)
    qt = qt_ref[...]
    dq_ref[...] = dq_in[...]
    for j in range(2):
        rows = slice(j * 512, (j + 1) * 512)
        s = s_ref[0, j : j + 1, :]
        dk, dv = grad_block(
            keys[j][...], values[j][...], qt, da, row_dot, s, e_ref, j, ds_ref, dq_ref, False
        )
        kv_ref[rows, k_cols] = dk
        kv_ref[rows, v_cols] = dv
    q_own[...] = (dq_ref[:, :512] * SCALE).T.astype(BF)
    q_send[...] = (dq_ref[:, 512:] * SCALE).T.astype(BF)


def near_grad_call(qt, da_own, da_recv, attn, scales, e_near, own, sib, dq):
    return pl.pallas_call(
        near_grad_kernel,
        grid=(2,),
        in_specs=[
            *common_specs(),
            pl.BlockSpec((1, 2, 512, 1024), lambda h: (h, 0, 0, 0)),
            *kv_specs(2),
            pl.BlockSpec((128, 1024), lambda h: (h, 0)),
        ],
        out_specs=[
            pl.BlockSpec((1024, 512), lambda h: (0, 0)),
            pl.BlockSpec((512, 128), lambda h: (0, h)),
            pl.BlockSpec((512, 128), lambda h: (0, h)),
        ],
        out_shape=[shape((1024, 512), F32), shape((512, 256)), shape((512, 256))],
        scratch_shapes=[pltpu.VMEM((512, 1024), BF), pltpu.VMEM((128, 1024), F32)],
        compiler_params=params(),
        cost_estimate=cost(4.8),
        name="near_grads",
    )(qt, da_own, da_recv, attn, scales, e_near, own, sib, own, sib, dq)


def spread(rows, level, refs, part):
    n = rows >> level
    wide = band(rows, n, 1 << level, 0.5**level, False)
    return [mm(wide, ref[part * n : (part + 1) * n, :], NN) for ref in refs]


def relay_kernel(side_ref, z1_ref, z3_ref, z2_ref, out_ref):
    parts = spread(512, 1, [z1_ref], 1) + spread(512, 2, [z3_ref, z2_ref], 1)
    out_ref[...] = functools.reduce(jnp.add, parts, side_ref[...].astype(F32)).astype(BF)


def relay_call(side, *along):
    return pl.pallas_call(
        relay_kernel,
        out_shape=shape((512, 512)),
        compiler_params=params(),
        cost_estimate=cost(0.6),
        name="relay",
    )(side, *along)


def collect_kernel(kv_ref, q_ref, side_ref, z1_ref, z3_ref, z2_ref, own_ref, send_k, send_v):
    send_k[:, 256:] = q_ref[:, :128]
    send_v[:, 256:] = q_ref[:, 128:]
    for part in (1, 0):
        start = kv_ref[part * 512 : (part + 1) * 512, :]
        parts = spread(512, 1, [side_ref], part)
        parts += spread(512, 2, [z1_ref.at[:256]], part)
        parts += spread(512, 3, [z3_ref.at[:128], z2_ref.at[:128]], part)
        done = functools.reduce(jnp.add, parts, start).astype(BF)
        if part:
            send_k[:, :256] = done[:, :256]
            send_v[:, :256] = done[:, 256:]
        else:
            own_ref[...] = done


def collect_call(kv_grad, q_send, side, *along):
    return pl.pallas_call(
        collect_kernel,
        out_shape=[shape((512, 512))] + [shape((512, 384))] * 2,
        compiler_params=params(),
        cost_estimate=cost(1.3),
        name="collect",
    )(kv_grad, q_send, side, *along)


def place_kernel(pos, q_own, kv_own, recv_k, recv_v, q_out, k_out, v_out):
    mine = pl.ds(pl.multiple_of(pos[0] * 256, 256), 256)
    other = pl.ds(pl.multiple_of((1 - pos[0]) * 256, 256), 256)
    q_out[:, mine] = q_own[...]
    base = pl.multiple_of((1 - pos[0]) * 256, 128)
    q_out[:, pl.ds(base, 128)] = recv_k[:, 256:]
    q_out[:, pl.ds(base + 128, 128)] = recv_v[:, 256:]
    k_out[:, mine] = kv_own[:, :256]
    k_out[:, other] = recv_k[:, :256]
    v_out[:, mine] = kv_own[:, 256:]
    v_out[:, other] = recv_v[:, :256]


def place_call(pos, q_own, kv_own, *recv):
    return pl.pallas_call(
        place_kernel,
        grid_spec=pltpu.PrefetchScalarGridSpec(
            num_scalar_prefetch=1,
            grid=(1,),
            in_specs=[whole(512, 256), whole(512, 512)] + [whole(512, 384)] * 2,
            out_specs=[whole(512, 512)] * 3,
        ),
        out_shape=[shape((512, 512))] * 3,
        compiler_params=params(),
        cost_estimate=cost(1.0),
        name="place",
    )(pos, q_own, kv_own, *recv)


def total(*terms):
    return functools.reduce(jnp.add, [t.astype(F32) for t in terms])


def cross_kernel(keep, c1, c3, o1, o3, out_ref):
    out_ref[:256, :] = total(keep[:256, :], c1[256:, :], o3[:256, :]).astype(BF)
    out_ref[256:, :] = total(keep[256:, :], c3[256:, :], o1[:256, :]).astype(BF)


def output_kernel(keep, o1, o3, end_1, end_3, cross, out_ref):
    out_ref[:256, :] = total(keep[:256, :], o1[512:, :], end_3[...], cross[:256, :]).astype(BF)
    out_ref[256:, :] = total(keep[256:, :], o3[512:, :], end_1[...], cross[256:, :]).astype(BF)


def weight_sum_kernel(own, wx, keep, first_1, first_3, late_1, late_3):
    def part(dz, half):
        return total(own[dz, half], wx[dz, half])

    keep[0] = part(0, 0)
    keep[1] = part(0, 1)
    first_1[0] = part(2, 0).astype(BF)
    first_1[1] = part(1, 0).astype(BF)
    first_3[0] = part(2, 1).astype(BF)
    first_3[1] = part(3, 1).astype(BF)
    late_1[...] = part(1, 1).astype(BF)
    late_3[...] = part(3, 0).astype(BF)


def weight_out_kernel(pos, keep, w1, w3, we_1, we_3, out_ref):
    up = total(keep[0], w1[1], we_3[...])
    down = total(keep[1], w3[1], we_1[...])
    for row, part in ((pos[0] * 256, up), ((1 - pos[0]) * 256, down)):
        out_ref[pl.ds(pl.multiple_of(row, 256), 256), :] = part.astype(BF)


def plain_call(kernel, out_shape, us, name, *args):
    return pl.pallas_call(
        kernel,
        out_shape=out_shape,
        compiler_params=params(),
        cost_estimate=cost(us),
        name=name,
    )(*args)


def weight_out_call(pos, *args):
    return pl.pallas_call(
        weight_out_kernel,
        grid_spec=pltpu.PrefetchScalarGridSpec(
            num_scalar_prefetch=1,
            grid=(1,),
            in_specs=[whole(2, 256, 256)] * 3 + [whole(256, 256)] * 2,
            out_specs=whole(512, 256),
        ),
        out_shape=shape((512, 256)),
        compiler_params=params(),
        cost_estimate=cost(1.0),
        name="weight_out",
    )(pos, *args)


def add(*terms):
    return functools.reduce(jnp.add, [t.astype(F32) for t in terms])


def after(values, *done):
    return lax.optimization_barrier((values, done))[0]


def low(*terms):
    return add(*terms).astype(BF)


def shards(queries, key_rows, value_rows, out_weight, output_grad):
    ctx = lax.axis_index("ctx")
    core = ctx % 2
    pos = jnp.stack([core, lax.axis_index("head"), ctx // 2]).astype(jnp.int32)

    k_recv, v_recv, q_recv = [swap(a, "ctx", 1) for a in (key_rows, value_rows, queries)]
    qt_own, kv_own, l1_own = prepare_call(pos, queries, key_rows, value_rows)
    k_recv, v_recv = after((k_recv, v_recv), q_recv)
    kv_sib, l1 = pool_call(pos, k_recv, v_recv, l1_own)
    side = swap(l1, "ctx", 2)
    l2, l3, qt = pool_more_call(pos, l1, qt_own, q_recv)
    along = [swap(a, "ctx", mask) for a, mask in ((l2, 4), (l3, 12), (l3, 8))]
    e_near, *carry = score_call(near_kernel, "near_scores", 4.2, qt, (kv_own, kv_sib), ())
    level = after(jnp.concatenate(along, axis=0), e_near, side)
    cross_level = swap(level, "ctx", 2)
    e_middle, *carry = score_call(
        middle_kernel, "middle_scores", 4.2, qt, (side, level), carry
    )
    da_own, da_send, grad_send = grad_attention_call(
        pos, *after((out_weight, output_grad), level)
    )
    cross_level = after(cross_level, da_own, e_middle)
    da_recv, grad_recv = [swap(a, "ctx", 1) for a in after((da_send, grad_send), cross_level)]
    e_last, attn, scales = score_call(
        last_kernel, "last_scores", 2.2, qt, (cross_level,), carry, True
    )
    far = (side, level, cross_level)

    attn_other = after(swap(attn, "ctx", 1), da_recv, grad_recv)
    first_c1, first_c3, late_c1, late_c3 = project_away_call(
        pos, attn, attn_other, out_weight, 1
    )
    got_c1, got_c3 = swap(first_c1, "head", 2), swap(first_c3, "head", 6)

    attn_v, other_v = after((attn, attn_other), first_c1)
    w_cross = weight_call(pos, attn_v, other_v, output_grad, grad_recv, 1)
    w_recv = swap(w_cross, "ctx", 2)

    attn_g, qt_g = after((attn, qt), w_cross)
    side_grad, *level_grads, dq = far_grad_call(
        qt_g, da_own, da_recv, attn_g, scales, e_middle, e_last, far
    )
    back = [swap(g, "ctx", mask) for g, mask in zip(level_grads[:2], (4, 12))]

    attn_p, other_p = after((attn, attn_other), side_grad)
    keep_o, first_o1, first_o3, late_o1, late_o3 = project_call(
        pos, attn_p, other_p, out_weight, 0
    )
    send_1 = jnp.concatenate([low(late_c1, got_c3[:256]), first_o1], axis=0)
    send_3 = jnp.concatenate([low(late_c3, got_c1[:256]), first_o3], axis=0)
    send_1, send_3 = after((send_1, send_3))
    got_o1, got_o3 = swap(send_1, "head", 2), swap(send_3, "head", 6)
    back.append(swap(after(level_grads[2], back[1]), "ctx", 8))
    attn_w, other_w = after((attn, attn_other), (keep_o, send_1, send_3))
    w_own = weight_call(pos, attn_w, other_w, output_grad, grad_recv, 0)
    qt_n, da_n = after((qt, da_own), w_own)
    kv_grad, q_own, q_send = near_grad_call(
        qt_n, da_n, da_recv, attn, scales, e_near, kv_own, kv_sib, dq
    )

    attn_k, other_k = after((attn, attn_other), kv_grad)
    keep_c = project_keep_call(pos, attn_k, other_k, out_weight, 1)
    relayed = relay_call(after(side_grad, send_1, send_3, keep_c), *back)
    side_back = swap(relayed, "ctx", 2)
    keep_w, first_w1, first_w3, late_w1, late_w3 = plain_call(
        weight_sum_kernel,
        [shape((2, 256, 256), F32)] + [shape((2, 256, 256))] * 2 + [shape((256, 256))] * 2,
        0.5,
        "weight_sum",
        *(after(w_own, relayed), w_recv),
    )
    got_w1, got_w3 = swap(first_w1, "ctx", 4), swap(first_w3, "ctx", 12)

    cross = plain_call(
        cross_kernel, shape((512, 512)), 1.0, "cross", keep_c, got_c1, got_c3, got_o1, got_o3
    )
    got_w1, got_w3 = after((got_w1, got_w3), (relayed, cross))
    cross_back = swap(cross, "head", 1)
    end_1 = swap(low(late_o1, got_o3[256:512]), "head", 2)
    end_3 = swap(low(late_o3, got_o1[256:512]), "head", 6)
    end_w1 = swap(low(late_w1, got_w3[0]), "ctx", 4)
    end_w3 = swap(low(late_w3, got_w1[0]), "ctx", 12)
    weight_grad = weight_out_call(pos, keep_w, got_w1, got_w3, end_w1, end_w3)

    layer_output = plain_call(
        output_kernel, shape((512, 512)), 1.0, "output", keep_o, got_o1, got_o3, end_1, end_3, cross_back
    )
    kv_done, *sends = collect_call(after(kv_grad, (end_w1, end_w3)), q_send, side_back, *back)
    query_grad, key_grad, value_grad = place_call(pos, q_own, kv_done, *[swap(a, "ctx", 1) for a in sends])
    return (layer_output, query_grad, key_grad, value_grad, weight_grad)


def solution(mesh):
    placed = (P("ctx", "head"), P("ctx", "head"), P("ctx", "head"), P("head", None), P("ctx", None))
    return jax.shard_map(
        shards,
        mesh=mesh,
        in_specs=placed,
        out_specs=(
            P("ctx", "head"),
            P("ctx", "head"),
            P("ctx", "head"),
            P("ctx", "head"),
            P("head", "ctx"),
        ),
        check_vma=False,
    )
```
